512 devices in a mesh: cube: 64 (over z_lo, x, core), col: 8 (over z_hi, y).
Axes of the slice: x: 4, y: 4, z: 16 (z_hi: 2, z_lo: 8; z = z_hi * 8 + z_lo), core: 2. Of those that a mesh axis runs over, the one named last changes fastest.
Arguments:
- front_matrix: float32 [12288, 12288], P('cube', 'col'), may hold values from -6 to 6
- child_tiles: bfloat16 [64, 8, 128, 32, 128], P('cube', 'col'), may hold values from -6 to 6
- dest_cube: int32 [64, 8, 128, 1], P('cube', 'col'), may hold values from 0 to 63; in each aligned block of 128 rows (0 to 127, 128 to 255, ..., all dimensions but the last counted through in order) at most 4 rows name the same one
- dest_slot: int32 [64, 8, 128], P('cube', 'col'), may hold values from 0 to 71
- diag_inverse: bfloat16 [512, 512], replicated, may hold values from -0.0546875 to 0.0546875
Outputs:
- factored: float32 [12288, 12288], P('cube', 'col')
The draws below stay inside these ranges and needn't reach their ends.
Inputs may be any that keep to these rules, and one draw needn't show every extreme that they name: `dest_cube`: among the tiles held by one device, at most 4 name the same row block, and every draw has a device where some row block is named exactly 4 times.
All inputs are finite; a program needn't handle non-finite values.
Results may differ from the reference program's by a relative error of at most 0.0043.
Values may be sent and summed in bfloat16 or wider, within the bound.
A program may use at most 64 MiB of HBM per device.

```python
import math
import jax
import jax.numpy as jnp
import numpy as np

NF = 12288
PW = 512
TR = 32
TC = 128
CAP = 4
CT = 128
LT = 72
N_CUBE = 64
N_COL = 8


def place_ends(values, key, low, high):
    dims = values.shape
    index_at = [jax.random.randint(jax.random.fold_in(key, axis), (), 0, dims[axis]) for axis in range(len(dims))]
    values = values.at[tuple(index_at)].set(low)
    longest = dims.index(max(dims))
    index_at[longest] = (index_at[longest] + 1) % dims[longest]
    return values.at[tuple(index_at)].set(high)


def level_of(stream_key, extent, shards, least, high):
    def one(axis_at, parts):
        draws = jax.random.uniform(jax.random.fold_in(jax.random.fold_in(stream_key, 6), axis_at), (parts,), jnp.float32, least / len(shards), high / len(shards))
        return jnp.repeat(jnp.exp(draws), extent[axis_at] // parts).reshape((-1,) + (1,) * (len(extent) - axis_at - 1))

    loudness = one(*shards[0])
    for cut in shards[1:]:
        loudness = loudness * one(*cut)
    return loudness


def deal_out(key, own, number, rows, count, top, most, slope):
    ranking = jax.random.permutation(key, count)
    crowded, usual = shares(count, rows * top, most, slope, True), shares(count, rows * top, most, slope, False)
    places = jnp.arange(count)

    def named(lengths, rotation):
        used = int((lengths > 0).sum())
        fixed = max(1, used // 4)
        passed = fixed + (places - fixed + rotation * (used - fixed)) % max(1, count - fixed)
        return jnp.zeros((count,), jnp.int32).at[ranking[jnp.where(places < fixed, places, passed)]].set(jnp.asarray(lengths, jnp.int32))

    lengths = jnp.where(number % 4 == 0, named(crowded, number // 4), named(usual, number - number // 4 - 1))
    mixed = jax.random.permutation(jax.random.fold_in(own, 3), count)
    donor, sink = mixed[0:count // 2 * 2:2], mixed[1:count // 2 * 2:2]
    slack = jnp.minimum(lengths[donor] - 1, most - lengths[sink]) // 2
    slack = jnp.where((donor == ranking[0]) | (sink == ranking[0]) | (lengths[sink] == 0), 0, jnp.maximum(slack, 0))
    passed = jax.random.randint(jax.random.fold_in(own, 4), (count // 2,), 0, 1 << 20) % (slack + 1)
    lengths = lengths.at[donor].add(-passed).at[sink].add(passed)
    members = jnp.searchsorted(jnp.cumsum(lengths), jnp.arange(rows * top), side="right").astype(jnp.int32)
    table = members.reshape(top, rows).T
    table = table[jax.random.permutation(jax.random.fold_in(own, 1), rows)]
    rotation = jax.random.randint(jax.random.fold_in(own, 2), (rows, 1), 0, top)
    return jnp.take_along_axis(table, (jnp.arange(top)[None, :] + rotation) % top, axis=1)


def shares(amount, total, most, slope, full):
    loads = [(1 << 20) // math.isqrt(grade ** slope) + 1 for grade in range(1, amount + 1)]
    largest = most if full else min(most, max(-(-total // amount), total * loads[0] // sum(loads)))
    least = 1 if total - largest >= amount - 1 else 0
    counts, surplus = [largest] + [least] * (amount - 1), total - largest - least * (amount - 1)
    while surplus > 0:
        movable = [i for i in range(1, amount) if counts[i] < largest] or [i for i in range(1, amount) if counts[i] < most]
        mass, left = sum([loads[i] for i in movable]), surplus
        for i in movable:
            extra = min(most - counts[i], max(1, left * loads[i] // mass), surplus)
            counts[i] = counts[i] + extra
            surplus = surplus - extra
    return np.array(counts)


def normal_values(rng, dims, scale, limit, pieces=(), kind=jnp.bfloat16):
    array = scale * jax.random.normal(rng, dims, jnp.float32)
    if pieces:
        array = array * level_of(rng, dims, pieces, -0.22, 0.18)
    return jnp.clip(array, -limit, limit).astype(kind)


def setup_inputs(seed: int = 0) -> dict:
    seeds = jax.random.split(jax.random.key(seed), 6)
    front_matrix = normal_values(seeds[0], (NF, NF), 1.0, 6.0, ((0, 64), (1, 8)), jnp.float32)
    child_tiles = normal_values(seeds[1], (N_CUBE, N_COL, CT, TR, TC), 1.0, 6.0, ((0, 64), (1, 8)))
    dest_cube_keys = jax.random.split(jax.random.fold_in(seeds[2], 1), N_CUBE * N_COL * CT // CT)
    dest_cube_turns = jax.random.permutation(jax.random.fold_in(seeds[2], 3), N_CUBE * N_COL * CT // CT)
    dest_cube = jax.vmap(lambda own, number: deal_out(jax.random.fold_in(seeds[2], 2), own, number, CT, N_CUBE, 1, CAP, 2))(dest_cube_keys, dest_cube_turns).reshape((N_CUBE, N_COL, CT, 1))
    dest_slot = place_ends(jax.random.randint(seeds[3], (N_CUBE, N_COL, CT), 0, LT), jax.random.fold_in(seeds[3], 1), 0, LT - 1).astype(jnp.int32)
    diag_inverse = normal_values(seeds[4], (PW, PW), (25 * PW) ** -0.5, 0.0546875)
    return dict(front_matrix=front_matrix, child_tiles=child_tiles, dest_cube=dest_cube, dest_slot=dest_slot, diag_inverse=diag_inverse)


def reference(front_matrix, child_tiles, dest_cube, dest_slot, diag_inverse):
    rows_local = NF // N_CUBE
    cols_local = NF // N_COL
    tile_cols = cols_local // TC
    grid_cols = NF // TC
    flat_tiles = child_tiles.astype(jnp.float32).reshape(N_CUBE * N_COL * CT, TR, TC)
    col_owner = jnp.broadcast_to(jnp.arange(N_COL, dtype=jnp.int32)[None, :, None], (N_CUBE, N_COL, CT)).reshape(-1)
    cube_to = dest_cube.reshape(-1).astype(jnp.int32)
    slot_ids = dest_slot.reshape(-1).astype(jnp.int32)
    grid_row = cube_to * (rows_local // TR) + slot_ids // tile_cols
    grid_col = col_owner * tile_cols + slot_ids % tile_cols
    segment = grid_row * grid_cols + grid_col
    summed = jax.ops.segment_sum(flat_tiles, segment, num_segments=(NF // TR) * grid_cols)
    placed = summed.reshape(NF // TR, grid_cols, TR, TC).transpose(0, 2, 1, 3).reshape(NF, NF)
    assembled = front_matrix + placed
    panel_in = assembled[:, :PW].astype(jnp.bfloat16)
    panel_factor = jnp.dot(panel_in, diag_inverse, preferred_element_type=jnp.float32).astype(jnp.bfloat16)
    update = jnp.dot(panel_factor, panel_factor[PW:].T, preferred_element_type=jnp.float32)
    trailing = assembled[:, PW:] - update
    return jnp.concatenate([panel_factor.astype(jnp.float32), trailing], axis=1)
```

```python
import functools

import jax
import jax.numpy as jnp
from jax import lax
from jax.experimental import pallas as pl
from jax.experimental.pallas import tpu as pltpu
from jax.sharding import PartitionSpec as P

CAP = 4
MESH = pl.DeviceIdType.MESH
QUARTERS = 4
MIDDLE = 4
BLOCKS = 8


def spread_kernel(
    assembled_ref,
    diag_ref,
    out_ref,
    own,
    across,
    own_recv,
    across_recv,
    down_send,
    cross_send,
    level_send,
    entry_send,
    chain_send,
    row_send,
    core_send,
):
    cube = lax.axis_index("cube")
    col = lax.axis_index("col")
    z = cube // 8
    x = (cube // 2) % 4
    core = cube % 2
    half = col // 4
    y = col % 4
    block = cube % 8
    rows, cols = assembled_ref.shape
    width = diag_ref.shape[0]
    depth = rows // QUARTERS

    def at(z_to, x_to, core_to, half_to, y_to):
        return {"cube": z_to * 8 + x_to * 2 + core_to, "col": half_to * 4 + y_to}

    is_root = col == 0
    is_entry = (half == 0) & (y == z % 4)
    is_middle = z == MIDDLE
    has_above = z < 7
    has_below = z > 0
    level_peers = [at(z, x, core, half, (y + s) % 4) for s in (1, 2, 3)]
    half_peer = at(z, x, core, 1 - half, y)
    row_peers = [at(z, (x + s) % 4, core, half, y) for s in (1, 2, 3)]
    core_peer = at(z, x, 1 - core, half, y)
    above = at(z + 1, x, core, half, y)
    below = at(z - 1, x, core, half, y)
    entry_to = at(MIDDLE, x, core, z // 4, y)
    entry_from = at(half * 4 + y, x, core, 0, y)

    barrier = pltpu.get_barrier_semaphore()

    def greet(device):
        pl.semaphore_signal(barrier, inc=1, device_id=device, device_id_type=MESH)

    for device in level_peers + [half_peer] + row_peers + [core_peer]:
        greet(device)
    for there, device in (
        (has_above, above),
        (has_below, below),
        (is_entry, entry_to),
        (is_middle, entry_from),
    ):
        pl.when(there)(functools.partial(greet, device))

    @pl.when(is_root)
    def _():
        panel = jnp.dot(
            assembled_ref[:, :width].astype(jnp.bfloat16),
            diag_ref[...],
            preferred_element_type=jnp.float32,
        ).astype(jnp.bfloat16)
        for q in range(QUARTERS):
            own[q] = panel[q * depth : (q + 1) * depth]

    pl.semaphore_wait(
        barrier,
        8
        + has_above.astype(jnp.int32)
        + has_below.astype(jnp.int32)
        + is_entry.astype(jnp.int32)
        + is_middle.astype(jnp.int32),
    )

    started = []

    def send(there, source, target, send_sem, recv_sem, device):
        copy = pltpu.make_async_remote_copy(
            src_ref=source,
            dst_ref=target,
            send_sem=send_sem,
            recv_sem=recv_sem,
            device_id=device,
            device_id_type=MESH,
        )
        if there is None:
            copy.start()
        else:
            pl.when(there)(copy.start)
        started.append((there, copy))

    def arrived(target, recv_sem):
        pltpu.make_async_remote_copy(
            src_ref=target,
            dst_ref=target,
            send_sem=recv_sem,
            recv_sem=recv_sem,
            device_id=core_peer,
            device_id_type=MESH,
        ).wait_recv()

    first = jnp.maximum(z % 4 - 1, 0)
    for s in range(3):
        y_to = 1 + (first + s) % 3
        for q in range(QUARTERS):
            send(
                is_root,
                own.at[q],
                own.at[q],
                down_send.at[s * QUARTERS + q],
                own_recv.at[q],
                at(z, x, core, 0, y_to),
            )

    for q in range(QUARTERS):
        pl.when((half == 0) & (y != 0))(functools.partial(arrived, own.at[q], own_recv.at[q]))
        send(
            is_entry,
            own.at[q],
            across.at[block, q],
            entry_send.at[q],
            across_recv.at[block, q],
            entry_to,
        )
    send(half == 0, own.at[y], own.at[y], cross_send.at[0], own_recv.at[y], half_peer)

    for q in range(QUARTERS):
        arrived(across.at[block, q], across_recv.at[block, q])
        mine = (across.at[block, q], across.at[block, q])
        ready = across_recv.at[block, q]
        send(has_above & (z >= MIDDLE), *mine, chain_send.at[q, 0], ready, above)
        send(has_below & (z <= MIDDLE), *mine, chain_send.at[q, 1], ready, below)
        for s in range(3):
            send(None, *mine, row_send.at[q, s], ready, row_peers[s])
        send(None, *mine, core_send.at[q, 0], ready, core_peer)
        if q == 1:
            pl.when(half == 1)(functools.partial(arrived, own.at[y], own_recv.at[y]))
            for s in range(3):
                send(
                    half == 1,
                    own.at[y],
                    own.at[y],
                    level_send.at[s],
                    own_recv.at[y],
                    level_peers[s],
                )
        for s in range(3):
            theirs = ((x + s + 1) % 4) * 2 + core
            arrived(across.at[theirs, q], across_recv.at[theirs, q])
            send(
                None,
                across.at[theirs, q],
                across.at[theirs, q],
                core_send.at[q, s + 1],
                across_recv.at[theirs, q],
                core_peer,
            )

    for s in range(1, QUARTERS):
        q = (y + s) % 4
        pl.when(half == 1)(functools.partial(arrived, own.at[q], own_recv.at[q]))
    for q in range(QUARTERS):
        for s in range(4):
            theirs = s * 2 + 1 - core
            arrived(across.at[theirs, q], across_recv.at[theirs, q])

    panel = own[...].reshape(rows, width)
    span = cols // 4
    for s in range(4):
        part = across[2 * s : 2 * s + 2].reshape(span, width)
        update = lax.dot_general(
            panel, part, (((1,), (1,)), ((), ())), preferred_element_type=jnp.float32
        )
        here = slice(s * span, (s + 1) * span)
        out_ref[:, here] = assembled_ref[:, here] - update

    @pl.when(is_root)
    def _():
        out_ref[:, :width] = panel.astype(jnp.float32)

    for there, copy in started:
        if there is None:
            copy.wait_send()
        else:
            pl.when(there)(copy.wait_send)


def spread(assembled, diag_inverse):
    rows, cols = assembled.shape
    width = diag_inverse.shape[0]
    depth = rows // QUARTERS
    vmem = pl.BlockSpec(memory_space=pltpu.VMEM)
    dma = pltpu.SemaphoreType.DMA
    return pl.pallas_call(
        spread_kernel,
        out_shape=jax.ShapeDtypeStruct((rows, cols), jnp.float32),
        in_specs=[vmem, vmem],
        out_specs=vmem,
        scratch_shapes=[
            pltpu.VMEM((QUARTERS, depth, width), jnp.bfloat16),
            pltpu.VMEM((BLOCKS, QUARTERS, depth, width), jnp.bfloat16),
            dma((QUARTERS,)),
            dma((BLOCKS, QUARTERS)),
            dma((3 * QUARTERS,)),
            dma((1,)),
            dma((3,)),
            dma((QUARTERS,)),
            dma((QUARTERS, 2)),
            dma((QUARTERS, 3)),
            dma((QUARTERS, 4)),
        ],
        compiler_params=pltpu.CompilerParams(
            collective_id=1, has_side_effects=True, vmem_limit_bytes=40 * 2**20
        ),
    )(assembled, diag_inverse)


def local(front_matrix, child_tiles, dest_cube, dest_slot, diag_inverse):
    cube_count = lax.axis_size("cube")
    rows_local, cols_local = front_matrix.shape
    tile_count = child_tiles.shape[2]
    tile_rows = child_tiles.shape[3]
    tile_width = child_tiles.shape[4]
    capacity = CAP
    tile_cols = cols_local // tile_width
    slots_local = rows_local // tile_rows * tile_cols
    flat_tiles = child_tiles.reshape(tile_count, tile_rows * tile_width)
    target = dest_cube.reshape(tile_count)
    slot_ids = dest_slot.reshape(tile_count)
    onehot = (target[:, None] == jnp.arange(cube_count, dtype=jnp.int32)[None, :]).astype(jnp.int32)
    before = jnp.cumsum(onehot, axis=0) - onehot
    position = jnp.sum(before * onehot, axis=1)
    buffer_row = target * capacity + position
    send_tiles = (
        jnp.zeros((cube_count * capacity, tile_rows * tile_width), jnp.bfloat16)
        .at[buffer_row]
        .set(flat_tiles)
    )
    send_slots = (
        jnp.full((cube_count * capacity,), slots_local, jnp.int32).at[buffer_row].set(slot_ids)
    )
    got_tiles, got_slots = (
        lax.all_to_all(
            send_tiles.reshape(cube_count, capacity, tile_rows * tile_width),
            "cube",
            split_axis=0,
            concat_axis=0,
            tiled=True,
        ),
        lax.all_to_all(
            send_slots.reshape(cube_count, capacity),
            "cube",
            split_axis=0,
            concat_axis=0,
            tiled=True,
        ),
    )
    got_tiles = got_tiles.reshape(cube_count * capacity, tile_rows * tile_width)
    got_slots = got_slots.reshape(cube_count * capacity)
    select = (jnp.arange(slots_local, dtype=jnp.int32)[:, None] == got_slots[None, :]).astype(
        jnp.bfloat16
    )
    extend_sum = jnp.dot(select, got_tiles, preferred_element_type=jnp.float32)
    extend_sum = (
        extend_sum.reshape(rows_local // tile_rows, tile_cols, tile_rows, tile_width)
        .transpose(0, 2, 1, 3)
        .reshape(rows_local, cols_local)
    )
    return spread(front_matrix + extend_sum, diag_inverse)


def solution(mesh):
    in_specs = (
        P("cube", "col"),
        P("cube", "col", None, None, None),
        P("cube", "col", None, None),
        P("cube", "col", None),
        P(),
    )
    out_specs = P("cube", "col")
    return jax.shard_map(local, mesh=mesh, in_specs=in_specs, out_specs=out_specs, check_vma=False)
```

```python
import functools

import jax
import jax.numpy as jnp
from jax import lax
from jax.experimental import pallas as pl
from jax.experimental.pallas import tpu as pltpu
from jax.sharding import PartitionSpec as P

CAP = 4
EMPTY = 72
MESH = pl.DeviceIdType.MESH
QUARTERS = 4
MIDDLE = 4
BLOCKS = 8


def spread_kernel(
    assembled_ref,
    diag_ref,
    out_ref,
    own,
    across,
    own_recv,
    across_recv,
    down_send,
    cross_send,
    level_send,
    entry_send,
    chain_send,
    row_send,
    core_send,
):
    cube = lax.axis_index("cube")
    col = lax.axis_index("col")
    z = cube // 8
    x = (cube // 2) % 4
    core = cube % 2
    half = col // 4
    y = col % 4
    block = cube % 8
    rows, cols = assembled_ref.shape
    width = diag_ref.shape[0]
    depth = rows // QUARTERS

    def at(z_to, x_to, core_to, half_to, y_to):
        return {"cube": z_to * 8 + x_to * 2 + core_to, "col": half_to * 4 + y_to}

    is_root = col == 0
    is_entry = (half == 0) & (y == z % 4)
    is_middle = z == MIDDLE
    has_above = z < 7
    has_below = z > 0
    level_peers = [at(z, x, core, half, (y + s) % 4) for s in (1, 2, 3)]
    half_peer = at(z, x, core, 1 - half, y)
    row_peers = [at(z, (x + s) % 4, core, half, y) for s in (1, 2, 3)]
    core_peer = at(z, x, 1 - core, half, y)
    above = at(z + 1, x, core, half, y)
    below = at(z - 1, x, core, half, y)
    entry_to = at(MIDDLE, x, core, z // 4, y)
    entry_from = at(half * 4 + y, x, core, 0, y)

    barrier = pltpu.get_barrier_semaphore()

    def greet(device):
        pl.semaphore_signal(barrier, inc=1, device_id=device, device_id_type=MESH)

    for device in level_peers + [half_peer] + row_peers + [core_peer]:
        greet(device)
    for there, device in (
        (has_above, above),
        (has_below, below),
        (is_entry, entry_to),
        (is_middle, entry_from),
    ):
        pl.when(there)(functools.partial(greet, device))

    @pl.when(is_root)
    def _():
        panel = jnp.dot(
            assembled_ref[:, :width].astype(jnp.bfloat16),
            diag_ref[...],
            preferred_element_type=jnp.float32,
        ).astype(jnp.bfloat16)
        for q in range(QUARTERS):
            own[q] = panel[q * depth : (q + 1) * depth]

    pl.semaphore_wait(
        barrier,
        8
        + has_above.astype(jnp.int32)
        + has_below.astype(jnp.int32)
        + is_entry.astype(jnp.int32)
        + is_middle.astype(jnp.int32),
    )

    started = []

    def send(there, source, target, send_sem, recv_sem, device):
        copy = pltpu.make_async_remote_copy(
            src_ref=source,
            dst_ref=target,
            send_sem=send_sem,
            recv_sem=recv_sem,
            device_id=device,
            device_id_type=MESH,
        )
        if there is None:
            copy.start()
        else:
            pl.when(there)(copy.start)
        started.append((there, copy))

    def arrived(target, recv_sem):
        pltpu.make_async_remote_copy(
            src_ref=target,
            dst_ref=target,
            send_sem=recv_sem,
            recv_sem=recv_sem,
            device_id=core_peer,
            device_id_type=MESH,
        ).wait_recv()

    first = jnp.maximum(z % 4 - 1, 0)
    for s in range(3):
        y_to = 1 + (first + s) % 3
        for q in range(QUARTERS):
            send(
                is_root,
                own.at[q],
                own.at[q],
                down_send.at[s * QUARTERS + q],
                own_recv.at[q],
                at(z, x, core, 0, y_to),
            )

    for q in range(QUARTERS):
        pl.when((half == 0) & (y != 0))(functools.partial(arrived, own.at[q], own_recv.at[q]))
        send(
            is_entry,
            own.at[q],
            across.at[block, q],
            entry_send.at[q],
            across_recv.at[block, q],
            entry_to,
        )
    send(half == 0, own.at[y], own.at[y], cross_send.at[0], own_recv.at[y], half_peer)

    for q in range(QUARTERS):
        arrived(across.at[block, q], across_recv.at[block, q])
        mine = (across.at[block, q], across.at[block, q])
        ready = across_recv.at[block, q]
        send(has_above & (z >= MIDDLE), *mine, chain_send.at[q, 0], ready, above)
        send(has_below & (z <= MIDDLE), *mine, chain_send.at[q, 1], ready, below)
        for s in range(3):
            send(None, *mine, row_send.at[q, s], ready, row_peers[s])
        send(None, *mine, core_send.at[q, 0], ready, core_peer)
        if q == 1:
            pl.when(half == 1)(functools.partial(arrived, own.at[y], own_recv.at[y]))
            for s in range(3):
                send(
                    half == 1,
                    own.at[y],
                    own.at[y],
                    level_send.at[s],
                    own_recv.at[y],
                    level_peers[s],
                )
        for s in range(3):
            theirs = ((x + s + 1) % 4) * 2 + core
            arrived(across.at[theirs, q], across_recv.at[theirs, q])
            send(
                None,
                across.at[theirs, q],
                across.at[theirs, q],
                core_send.at[q, s + 1],
                across_recv.at[theirs, q],
                core_peer,
            )

    for s in range(1, QUARTERS):
        q = (y + s) % 4
        pl.when(half == 1)(functools.partial(arrived, own.at[q], own_recv.at[q]))
    for q in range(QUARTERS):
        for s in range(4):
            theirs = s * 2 + 1 - core
            arrived(across.at[theirs, q], across_recv.at[theirs, q])

    panel = own[...].reshape(rows, width)
    span = cols // 4
    for s in range(4):
        part = across[2 * s : 2 * s + 2].reshape(span, width)
        update = lax.dot_general(
            panel, part, (((1,), (1,)), ((), ())), preferred_element_type=jnp.float32
        )
        here = slice(s * span, (s + 1) * span)
        out_ref[:, here] = assembled_ref[:, here] - update

    @pl.when(is_root)
    def _():
        out_ref[:, :width] = panel.astype(jnp.float32)

    for there, copy in started:
        if there is None:
            copy.wait_send()
        else:
            pl.when(there)(copy.wait_send)


def spread(assembled, diag_inverse):
    rows, cols = assembled.shape
    width = diag_inverse.shape[0]
    depth = rows // QUARTERS
    vmem = pl.BlockSpec(memory_space=pltpu.VMEM)
    dma = pltpu.SemaphoreType.DMA
    return pl.pallas_call(
        spread_kernel,
        out_shape=jax.ShapeDtypeStruct((rows, cols), jnp.float32),
        in_specs=[vmem, vmem],
        out_specs=vmem,
        scratch_shapes=[
            pltpu.VMEM((QUARTERS, depth, width), jnp.bfloat16),
            pltpu.VMEM((BLOCKS, QUARTERS, depth, width), jnp.bfloat16),
            dma((QUARTERS,)),
            dma((BLOCKS, QUARTERS)),
            dma((3 * QUARTERS,)),
            dma((1,)),
            dma((3,)),
            dma((QUARTERS,)),
            dma((QUARTERS, 2)),
            dma((QUARTERS, 3)),
            dma((QUARTERS, 4)),
        ],
        compiler_params=pltpu.CompilerParams(
            collective_id=1, has_side_effects=True, vmem_limit_bytes=40 * 2**20
        ),
    )(assembled, diag_inverse)


def pack_kernel(cube_ref, slot_ref, tiles_ref, send_ref, slots_ref, counts):
    groups = send_ref.shape[0]
    slots_ref[...] = jnp.full(slots_ref.shape, EMPTY, jnp.int32)
    lane = lax.broadcasted_iota(jnp.int32, (1, slots_ref.shape[2]), 1)

    def clear(g, carry):
        counts[g] = 0
        return carry

    lax.fori_loop(0, groups, clear, 0, unroll=8)

    def place(t, carry):
        g = cube_ref[t]
        p = counts[g]
        counts[g] = p + 1
        send_ref[g, p] = tiles_ref[t]
        slots_ref[g] = jnp.where(lane == p, slot_ref[t], slots_ref[g])
        return carry

    lax.fori_loop(0, tiles_ref.shape[0], place, 0, unroll=4)


def pack(target, slot_ids, tiles, groups):
    smem = pl.BlockSpec(memory_space=pltpu.SMEM)
    vmem = pl.BlockSpec(memory_space=pltpu.VMEM)
    return pl.pallas_call(
        pack_kernel,
        out_shape=(
            jax.ShapeDtypeStruct((groups, CAP) + tiles.shape[1:], tiles.dtype),
            jax.ShapeDtypeStruct((groups, 1, 128), jnp.int32),
        ),
        in_specs=[smem, smem, vmem],
        out_specs=(vmem, vmem),
        scratch_shapes=[pltpu.SMEM((groups,), jnp.int32)],
        compiler_params=pltpu.CompilerParams(vmem_limit_bytes=40 * 2**20),
    )(target, slot_ids, tiles)


def exchange_kernel(
    send_ref, slots_ref, got_ref, got_slots_ref, tile_send, tile_recv, slot_send, slot_recv, self_sem
):
    groups = send_ref.shape[0]
    me = lax.axis_index("cube")
    barrier = pltpu.get_barrier_semaphore()

    def partner(step):
        return me ^ ((step % 8) * 8 + step // 8)

    def greet(step, carry):
        pl.semaphore_signal(
            barrier, inc=1, device_id={"cube": partner(step)}, device_id_type=MESH
        )
        return carry

    lax.fori_loop(1, groups, greet, 0)
    kept = pltpu.make_async_copy(send_ref.at[me], got_ref.at[me], self_sem.at[0])
    kept_slots = pltpu.make_async_copy(slots_ref.at[me], got_slots_ref.at[me], self_sem.at[1])
    kept.start()
    kept_slots.start()
    pl.semaphore_wait(barrier, groups - 1)

    def copies(step):
        to = partner(step)
        return (
            pltpu.make_async_remote_copy(
                src_ref=slots_ref.at[to],
                dst_ref=got_slots_ref.at[me],
                send_sem=slot_send.at[step],
                recv_sem=slot_recv.at[step],
                device_id={"cube": to},
                device_id_type=MESH,
            ),
            pltpu.make_async_remote_copy(
                src_ref=send_ref.at[to],
                dst_ref=got_ref.at[me],
                send_sem=tile_send.at[step],
                recv_sem=tile_recv.at[step],
                device_id={"cube": to},
                device_id_type=MESH,
            ),
        )

    def start(step, carry):
        for copy in copies(step):
            copy.start()
        return carry

    lax.fori_loop(1, groups, start, 0)

    def finish(step, carry):
        for copy in copies(step):
            copy.wait()
        return carry

    lax.fori_loop(1, groups, finish, 0)
    kept.wait()
    kept_slots.wait()


def exchange(send_tiles, send_slots):
    groups = send_tiles.shape[0]
    anywhere = pl.BlockSpec(memory_space=pl.ANY)
    dma = pltpu.SemaphoreType.DMA
    return pl.pallas_call(
        exchange_kernel,
        out_shape=(
            jax.ShapeDtypeStruct(send_tiles.shape, send_tiles.dtype),
            jax.ShapeDtypeStruct(send_slots.shape, send_slots.dtype),
        ),
        in_specs=[anywhere, anywhere],
        out_specs=(anywhere, anywhere),
        scratch_shapes=[
            dma((groups,)),
            dma((groups,)),
            dma((groups,)),
            dma((groups,)),
            dma((2,)),
        ],
        compiler_params=pltpu.CompilerParams(collective_id=2, has_side_effects=True),
    )(send_tiles, send_slots)


def add_kernel(slots_ref, front_ref, got_ref, out_ref, sums):
    groups, capacity, height, width = got_ref.shape
    rows, cols = front_ref.shape
    places = [
        (slice(r * height, (r + 1) * height), slice(c * width, (c + 1) * width))
        for r in range(rows // height)
        for c in range(cols // width)
    ]
    for s, place in enumerate(places):
        sums[s] = front_ref[place]

    def add(g, carry):
        for p in range(capacity):
            s = slots_ref[g, 0, p]
            sums[s] += got_ref[g, p].astype(jnp.float32)
        return carry

    lax.fori_loop(0, groups, add, 0, unroll=2)
    for s, place in enumerate(places):
        out_ref[place] = sums[s]


def extend_add(front, got_tiles, got_slots):
    smem = pl.BlockSpec(memory_space=pltpu.SMEM)
    vmem = pl.BlockSpec(memory_space=pltpu.VMEM)
    return pl.pallas_call(
        add_kernel,
        out_shape=jax.ShapeDtypeStruct(front.shape, front.dtype),
        in_specs=[smem, vmem, vmem],
        out_specs=vmem,
        scratch_shapes=[pltpu.VMEM((EMPTY + 1,) + got_tiles.shape[2:], jnp.float32)],
        compiler_params=pltpu.CompilerParams(vmem_limit_bytes=40 * 2**20),
    )(got_slots, front, got_tiles)


def local(front_matrix, child_tiles, dest_cube, dest_slot, diag_inverse):
    tile_count = child_tiles.shape[2]
    send_tiles, send_slots = pack(
        dest_cube.reshape(tile_count),
        dest_slot.reshape(tile_count),
        child_tiles.reshape(child_tiles.shape[2:]),
        lax.axis_size("cube"),
    )
    got_tiles, got_slots = exchange(send_tiles, send_slots)
    return spread(extend_add(front_matrix, got_tiles, got_slots), diag_inverse)


def solution(mesh):
    in_specs = (
        P("cube", "col"),
        P("cube", "col", None, None, None),
        P("cube", "col", None, None),
        P("cube", "col", None),
        P(),
    )
    out_specs = P("cube", "col")
    return jax.shard_map(local, mesh=mesh, in_specs=in_specs, out_specs=out_specs, check_vma=False)
```

```python
import functools

import jax
import jax.numpy as jnp
from jax import lax
from jax.experimental import pallas as pl
from jax.experimental.pallas import tpu as pltpu
from jax.sharding import PartitionSpec as P

CAP = 4
EMPTY = 72
HALF = 32
PARTS = 3
MESH = pl.DeviceIdType.MESH
QUARTERS = 4
MIDDLE = 4
BLOCKS = 8


def pack_kernel(cube_ref, slot_ref, tiles_ref, send_ref, slots_ref, counts):
    groups = send_ref.shape[0]
    place_from = (lax.axis_index("cube") % HALF) * CAP
    lane = lax.broadcasted_iota(jnp.int32, slots_ref.shape, 2)
    slots_ref[...] = jnp.where((lane >= place_from) & (lane < place_from + CAP), EMPTY, 0)
    lane = lax.broadcasted_iota(jnp.int32, (1, slots_ref.shape[2]), 1)

    def clear(g, carry):
        counts[g] = 0
        return carry

    lax.fori_loop(0, groups, clear, 0, unroll=8)

    def place(t, carry):
        g = cube_ref[t]
        p = counts[g]
        counts[g] = p + 1
        send_ref[g, p] = tiles_ref[t]
        slots_ref[g] = jnp.where(lane == place_from + p, slot_ref[t], slots_ref[g])
        return carry

    lax.fori_loop(0, tiles_ref.shape[0], place, 0, unroll=4)


def pack(target, slot_ids, tiles, groups):
    smem = pl.BlockSpec(memory_space=pltpu.SMEM)
    vmem = pl.BlockSpec(memory_space=pltpu.VMEM)
    return pl.pallas_call(
        pack_kernel,
        out_shape=(
            jax.ShapeDtypeStruct((groups, CAP) + tiles.shape[1:], tiles.dtype),
            jax.ShapeDtypeStruct((groups, 1, 128), jnp.int32),
        ),
        in_specs=[smem, smem, vmem],
        out_specs=(vmem, vmem),
        scratch_shapes=[pltpu.SMEM((groups,), jnp.int32)],
        compiler_params=pltpu.CompilerParams(vmem_limit_bytes=40 * 2**20),
    )(target, slot_ids, tiles)


def sort_table(row):
    count = row.shape[1]
    along = jnp.broadcast_to(row, (count, count))
    i = lax.broadcasted_iota(jnp.int32, (count, count), 0)
    j = lax.broadcasted_iota(jnp.int32, (count, count), 1)

    def total(mask, value, axis):
        return jnp.sum(jnp.where(mask, value, 0), axis=axis, keepdims=True)

    down = total(i == j, along, 1)
    earlier = (along == down) & (j < i)
    rank = total((along < down) | earlier, 1, 1)
    repeats = total(earlier, 1, 1)
    hit = rank == j
    return (
        total(hit, i, 0),
        total(hit & (repeats > 0), 1, 0),
        jnp.maximum(total(down <= j, 1, 0) - 1, 0),
        total(down == j, 1, 0),
    )


def front_kernel(
    send_ref,
    slots_ref,
    front_ref,
    diag_ref,
    out_ref,
    far_tiles,
    near_tiles,
    far_slots,
    near_slots,
    runs,
    table,
    order,
    dense,
    got_dense,
    own,
    across,
    table_sem,
    keep_sem,
    far_send,
    far_recv,
    far_slot_send,
    far_slot_recv,
    near_send,
    near_recv,
    near_slot_send,
    near_slot_recv,
    dense_send,
    dense_recv,
    own_recv,
    across_recv,
    down_send,
    cross_send,
    level_send,
    entry_send,
    chain_send,
    row_send,
    core_send,
):
    cube = lax.axis_index("cube")
    col = lax.axis_index("col")
    z = cube // 8
    x = (cube // 2) % 4
    core = cube % 2
    half = col // 4
    y = col % 4
    block = cube % 8
    near = cube % HALF
    base = cube - near
    mirror = cube ^ HALF
    rows, cols = front_ref.shape
    width = diag_ref.shape[0]
    depth = rows // QUARTERS
    tile_count, height, lanes = far_tiles.shape

    def at(z_to, x_to, core_to, half_to, y_to):
        return {"cube": z_to * 8 + x_to * 2 + core_to, "col": half_to * 4 + y_to}

    is_root = col == 0
    is_entry = (half == 0) & (y == z % 4)
    is_middle = z == MIDDLE
    has_above = z < 7
    has_below = z > 0
    level_peers = [at(z, x, core, half, (y + s) % 4) for s in (1, 2, 3)]
    half_peer = at(z, x, core, 1 - half, y)
    row_peers = [at(z, (x + s) % 4, core, half, y) for s in (1, 2, 3)]
    core_peer = at(z, x, 1 - core, half, y)
    above = at(z + 1, x, core, half, y)
    below = at(z - 1, x, core, half, y)
    entry_to = at(MIDDLE, x, core, z // 4, y)
    entry_from = at(half * 4 + y, x, core, 0, y)

    barrier = pltpu.get_barrier_semaphore()

    def greet(device):
        pl.semaphore_signal(barrier, inc=1, device_id=device, device_id_type=MESH)

    def near_peer(step):
        return base + (near ^ ((step % 4) * 8 + step // 4))

    def greet_near(step, carry):
        greet({"cube": near_peer(step)})
        return carry

    lax.fori_loop(1, HALF, greet_near, 0)
    for device in level_peers + [half_peer, {"cube": mirror}]:
        greet(device)
    for there, device in (
        (has_above, above),
        (has_below, below),
        (is_entry, entry_to),
        (is_middle, entry_from),
    ):
        pl.when(there)(functools.partial(greet, device))

    mine = pl.ds(near * CAP, CAP)
    kept = [
        pltpu.make_async_copy(send_ref.at[mirror], far_tiles.at[mine], keep_sem.at[0]),
        pltpu.make_async_copy(slots_ref.at[mirror], far_slots.at[near], keep_sem.at[1]),
        pltpu.make_async_copy(send_ref.at[cube], near_tiles.at[mine], keep_sem.at[2]),
        pltpu.make_async_copy(slots_ref.at[cube], near_slots.at[near], keep_sem.at[3]),
    ]
    for copy in kept:
        copy.start()

    pl.semaphore_wait(
        barrier,
        HALF
        + 4
        + has_above.astype(jnp.int32)
        + has_below.astype(jnp.int32)
        + is_entry.astype(jnp.int32)
        + is_middle.astype(jnp.int32),
    )

    def remote(source, target, send_sem, recv_sem, device):
        return pltpu.make_async_remote_copy(
            src_ref=source,
            dst_ref=target,
            send_sem=send_sem,
            recv_sem=recv_sem,
            device_id=device,
            device_id_type=MESH,
        )

    def far_copies(step):
        to = near_peer(step)
        device = {"cube": to}
        return (
            remote(
                slots_ref.at[to ^ HALF],
                far_slots.at[near],
                far_slot_send.at[step],
                far_slot_recv.at[step],
                device,
            ),
            remote(
                send_ref.at[to ^ HALF],
                far_tiles.at[mine],
                far_send.at[step],
                far_recv.at[step],
                device,
            ),
        )

    def near_copies(step):
        to = near_peer(step)
        device = {"cube": to}
        return (
            remote(
                slots_ref.at[to],
                near_slots.at[near],
                near_slot_send.at[step],
                near_slot_recv.at[step],
                device,
            ),
            remote(
                send_ref.at[to],
                near_tiles.at[mine],
                near_send.at[step],
                near_recv.at[step],
                device,
            ),
        )

    def each(copies, action):
        def body(step, carry):
            for copy in copies(step):
                getattr(copy, action)()
            return carry

        lax.fori_loop(1, HALF, body, 0)

    def sum_runs(slot_rows, tiles):
        for k, values in enumerate(sort_table(jnp.sum(slot_rows[...], axis=0))):
            table[k : k + 1] = values
        copy = pltpu.make_async_copy(table, order, table_sem.at[0])
        copy.start()
        copy.wait()

        def add(rank, run):
            tile = tiles[order[0, rank]].astype(jnp.float32)
            run = tile + jnp.where(order[1, rank] > 0, run, 0.0)
            runs[rank] = run
            return run

        lax.fori_loop(
            0, tile_count, add, jnp.zeros((height, lanes), jnp.float32), unroll=8
        )

    def block_sum(s):
        return jnp.where(order[3, s] > 0, runs[order[2, s]], 0.0)

    each(far_copies, "start")
    each(far_copies, "wait_recv")
    kept[0].wait()
    kept[1].wait()
    each(near_copies, "start")

    sum_runs(far_slots, far_tiles)
    per_row = cols // lanes
    group = width // lanes
    tile_rows = rows // height
    dense_copies = []
    for part in range(PARTS):

        def fill(r, carry):
            for c in range(group):
                dense[part, r * group + c] = block_sum(r * per_row + part * group + c).astype(
                    jnp.bfloat16
                )
            return carry

        lax.fori_loop(0, tile_rows, fill, 0, unroll=2)
        copy = remote(
            dense.at[part],
            got_dense.at[part],
            dense_send.at[part],
            dense_recv.at[part],
            {"cube": mirror},
        )
        copy.start()
        dense_copies.append(copy)

    each(near_copies, "wait_recv")
    kept[2].wait()
    kept[3].wait()
    sum_runs(near_slots, near_tiles)

    def assemble(part):
        dense_copies[part].wait_recv()

        def fill(r, carry):
            for c in range(group):
                here = (
                    pl.ds(pl.multiple_of(r * height, height), height),
                    pl.ds((part * group + c) * lanes, lanes),
                )
                out_ref[here] = (
                    front_ref[here]
                    + block_sum(r * per_row + part * group + c)
                    + got_dense[part, r * group + c].astype(jnp.float32)
                )
            return carry

        lax.fori_loop(0, tile_rows, fill, 0, unroll=2)

    assemble(0)

    @pl.when(is_root)
    def _():
        panel = jnp.dot(
            out_ref[:, :width].astype(jnp.bfloat16),
            diag_ref[...],
            preferred_element_type=jnp.float32,
        ).astype(jnp.bfloat16)
        for q in range(QUARTERS):
            own[q] = panel[q * depth : (q + 1) * depth]

    started = []

    def send(there, source, target, send_sem, recv_sem, device):
        copy = remote(source, target, send_sem, recv_sem, device)
        if there is None:
            copy.start()
        else:
            pl.when(there)(copy.start)
        started.append((there, copy))

    def arrived(target, recv_sem):
        remote(target, target, recv_sem, recv_sem, core_peer).wait_recv()

    first = jnp.maximum(z % 4 - 1, 0)
    for s in range(3):
        y_to = 1 + (first + s) % 3
        for q in range(QUARTERS):
            send(
                is_root,
                own.at[q],
                own.at[q],
                down_send.at[s * QUARTERS + q],
                own_recv.at[q],
                at(z, x, core, 0, y_to),
            )

    for q in range(QUARTERS):
        pl.when((half == 0) & (y != 0))(functools.partial(arrived, own.at[q], own_recv.at[q]))
        send(
            is_entry,
            own.at[q],
            across.at[block, q],
            entry_send.at[q],
            across_recv.at[block, q],
            entry_to,
        )
    send(half == 0, own.at[y], own.at[y], cross_send.at[0], own_recv.at[y], half_peer)

    for q in range(QUARTERS + 1):
        if q < QUARTERS:
            arrived(across.at[block, q], across_recv.at[block, q])
            held = (across.at[block, q], across.at[block, q])
            ready = across_recv.at[block, q]
            send(has_above & (z >= MIDDLE), *held, chain_send.at[q, 0], ready, above)
            send(has_below & (z <= MIDDLE), *held, chain_send.at[q, 1], ready, below)
            for s in range(3):
                send(None, *held, row_send.at[q, s], ready, row_peers[s])
            send(None, *held, core_send.at[q, 0], ready, core_peer)
        if q == 2:
            pl.when(half == 1)(functools.partial(arrived, own.at[y], own_recv.at[y]))
            for s in range(3):
                send(
                    half == 1,
                    own.at[y],
                    own.at[y],
                    level_send.at[s],
                    own_recv.at[y],
                    level_peers[s],
                )
        if q > 0:
            for s in range(3):
                theirs = ((x + s + 1) % 4) * 2 + core
                arrived(across.at[theirs, q - 1], across_recv.at[theirs, q - 1])
                send(
                    None,
                    across.at[theirs, q - 1],
                    across.at[theirs, q - 1],
                    core_send.at[q - 1, s + 1],
                    across_recv.at[theirs, q - 1],
                    core_peer,
                )

    for part in range(1, PARTS):
        assemble(part)
    for s in range(1, QUARTERS):
        q = (y + s) % 4
        pl.when(half == 1)(functools.partial(arrived, own.at[q], own_recv.at[q]))
    for q in range(QUARTERS):
        for s in range(4):
            theirs = s * 2 + 1 - core
            arrived(across.at[theirs, q], across_recv.at[theirs, q])

    panel = own[...].reshape(rows, width)
    span = cols // 4
    for s in range(4):
        part = across[2 * s : 2 * s + 2].reshape(span, width)
        update = lax.dot_general(
            panel, part, (((1,), (1,)), ((), ())), preferred_element_type=jnp.float32
        )
        here = slice(s * span, (s + 1) * span)
        out_ref[:, here] = out_ref[:, here] - update

    @pl.when(is_root)
    def _():
        out_ref[:, :width] = panel.astype(jnp.float32)

    each(far_copies, "wait_send")
    each(near_copies, "wait_send")
    for copy in dense_copies:
        copy.wait_send()
    for there, copy in started:
        if there is None:
            copy.wait_send()
        else:
            pl.when(there)(copy.wait_send)


def factor(send_tiles, send_slots, front, diag_inverse):
    rows, cols = front.shape
    width = diag_inverse.shape[0]
    depth = rows // QUARTERS
    tile = send_tiles.shape[2:]
    vmem = pl.BlockSpec(memory_space=pltpu.VMEM)
    dma = pltpu.SemaphoreType.DMA
    return pl.pallas_call(
        front_kernel,
        out_shape=jax.ShapeDtypeStruct((rows, cols), jnp.float32),
        in_specs=[vmem, vmem, vmem, vmem],
        out_specs=vmem,
        scratch_shapes=[
            pltpu.VMEM((HALF * CAP,) + tile, jnp.bfloat16),
            pltpu.VMEM((HALF * CAP,) + tile, jnp.bfloat16),
            pltpu.VMEM((HALF, 1, 128), jnp.int32),
            pltpu.VMEM((HALF, 1, 128), jnp.int32),
            pltpu.VMEM((HALF * CAP,) + tile, jnp.float32),
            pltpu.VMEM((8, 128), jnp.int32),
            pltpu.SMEM((8, 128), jnp.int32),
            pltpu.VMEM((PARTS, EMPTY // PARTS) + tile, jnp.bfloat16),
            pltpu.VMEM((PARTS, EMPTY // PARTS) + tile, jnp.bfloat16),
            pltpu.VMEM((QUARTERS, depth, width), jnp.bfloat16),
            pltpu.VMEM((BLOCKS, QUARTERS, depth, width), jnp.bfloat16),
            dma((1,)),
            dma((4,)),
            dma((HALF,)),
            dma((HALF,)),
            dma((HALF,)),
            dma((HALF,)),
            dma((HALF,)),
            dma((HALF,)),
            dma((HALF,)),
            dma((HALF,)),
            dma((PARTS,)),
            dma((PARTS,)),
            dma((QUARTERS,)),
            dma((BLOCKS, QUARTERS)),
            dma((3 * QUARTERS,)),
            dma((1,)),
            dma((3,)),
            dma((QUARTERS,)),
            dma((QUARTERS, 2)),
            dma((QUARTERS, 3)),
            dma((QUARTERS, 4)),
        ],
        compiler_params=pltpu.CompilerParams(
            collective_id=1, has_side_effects=True, vmem_limit_bytes=48 * 2**20
        ),
    )(send_tiles, send_slots, front, diag_inverse)


def local(front_matrix, child_tiles, dest_cube, dest_slot, diag_inverse):
    tile_count = child_tiles.shape[2]
    send_tiles, send_slots = pack(
        dest_cube.reshape(tile_count),
        dest_slot.reshape(tile_count),
        child_tiles.reshape(child_tiles.shape[2:]),
        lax.axis_size("cube"),
    )
    return factor(send_tiles, send_slots, front_matrix, diag_inverse)


def solution(mesh):
    in_specs = (
        P("cube", "col"),
        P("cube", "col", None, None, None),
        P("cube", "col", None, None),
        P("cube", "col", None),
        P(),
    )
    out_specs = P("cube", "col")
    return jax.shard_map(local, mesh=mesh, in_specs=in_specs, out_specs=out_specs, check_vma=False)
```

```python
import functools

import jax
import jax.numpy as jnp
from jax import lax
from jax.experimental import pallas as pl
from jax.experimental.pallas import tpu as pltpu
from jax.sharding import PartitionSpec as P

CAP = 4
EMPTY = 72
HALF = 32
PARTS = 3
MESH = pl.DeviceIdType.MESH
PIECES = 4
BURST = 4
EARLY = 2
LATE = 2
BLOCKS = 8


def pack_kernel(cube_ref, slot_ref, tiles_ref, send_ref, slots_ref, counts):
    groups = send_ref.shape[0]
    place_from = (lax.axis_index("cube") % HALF) * CAP
    lane = lax.broadcasted_iota(jnp.int32, slots_ref.shape, 2)
    slots_ref[...] = jnp.where((lane >= place_from) & (lane < place_from + CAP), EMPTY, 0)
    lane = lax.broadcasted_iota(jnp.int32, (1, slots_ref.shape[2]), 1)

    def clear(g, carry):
        counts[g] = 0
        return carry

    lax.fori_loop(0, groups, clear, 0, unroll=8)

    def place(t, carry):
        g = cube_ref[t]
        p = counts[g]
        counts[g] = p + 1
        send_ref[g, p] = tiles_ref[t]
        slots_ref[g] = jnp.where(lane == place_from + p, slot_ref[t], slots_ref[g])
        return carry

    lax.fori_loop(0, tiles_ref.shape[0], place, 0, unroll=4)


def pack(target, slot_ids, tiles, groups):
    smem = pl.BlockSpec(memory_space=pltpu.SMEM)
    vmem = pl.BlockSpec(memory_space=pltpu.VMEM)
    return pl.pallas_call(
        pack_kernel,
        out_shape=(
            jax.ShapeDtypeStruct((groups, CAP) + tiles.shape[1:], tiles.dtype),
            jax.ShapeDtypeStruct((groups, 1, 128), jnp.int32),
        ),
        in_specs=[smem, smem, vmem],
        out_specs=(vmem, vmem),
        scratch_shapes=[pltpu.SMEM((groups,), jnp.int32)],
        compiler_params=pltpu.CompilerParams(vmem_limit_bytes=40 * 2**20),
    )(target, slot_ids, tiles)


def sort_table(row):
    count = row.shape[1]
    along = jnp.broadcast_to(row, (count, count))
    i = lax.broadcasted_iota(jnp.int32, (count, count), 0)
    j = lax.broadcasted_iota(jnp.int32, (count, count), 1)

    def total(mask, value, axis):
        return jnp.sum(jnp.where(mask, value, 0), axis=axis, keepdims=True)

    down = total(i == j, along, 1)
    earlier = (along == down) & (j < i)
    rank = total((along < down) | earlier, 1, 1)
    repeats = total(earlier, 1, 1)
    hit = rank == j
    return (
        total(hit, i, 0),
        total(hit & (repeats > 0), 1, 0),
        jnp.maximum(total(down <= j, 1, 0) - 1, 0),
        total(down == j, 1, 0),
    )


def front_kernel(
    send_ref,
    slots_ref,
    front_ref,
    diag_ref,
    out_ref,
    far_tiles,
    near_tiles,
    far_slots,
    near_slots,
    runs,
    table,
    order,
    dense,
    got_dense,
    own,
    across,
    table_sem,
    keep_sem,
    far_send,
    far_recv,
    far_slot_send,
    far_slot_recv,
    near_send,
    near_recv,
    near_slot_send,
    near_slot_recv,
    dense_send,
    dense_recv,
    own_recv,
    across_recv,
    down_send,
    cross_send,
    level_send,
    entry_send,
    line_send,
    row_send,
    core_send,
):
    cube = lax.axis_index("cube")
    col = lax.axis_index("col")
    z = cube // 8
    x = (cube // 2) % 4
    core = cube % 2
    half = col // 4
    y = col % 4
    block = cube % 8
    near = cube % HALF
    base = cube - near
    mirror = cube ^ HALF
    rows, cols = front_ref.shape
    width = diag_ref.shape[0]
    depth = rows // PIECES
    tile_count, height, lanes = far_tiles.shape

    def at(z_to, x_to, core_to, half_to, y_to):
        return {"cube": z_to * 8 + x_to * 2 + core_to, "col": half_to * 4 + y_to}

    is_root = col == 0
    is_entry = (half == 0) & (y == z % 4)
    line = z - z % 4
    is_hub = z == jnp.where(z < 4, 2 - (col == 2).astype(jnp.int32), 5)
    level_peers = [at(z, x, core, half, (y + s) % 4) for s in (1, 2, 3)]
    half_peer = at(z, x, core, 1 - half, y)
    row_peers = [at(z, (x + s) % 4, core, half, y) for s in (1, 2, 3)]
    core_peer = at(z, x, 1 - core, half, y)
    line_peers = [at(line + (z + s) % 4, x, core, half, y) for s in (1, 2, 3)]
    entry_to = [
        at(hub, x, core, z // 4, y) for hub in (2 - (z == 2).astype(jnp.int32), 5)
    ]
    entry_from = at(half * 4 + y, x, core, 0, y)

    barrier = pltpu.get_barrier_semaphore()

    def greet(device):
        pl.semaphore_signal(barrier, inc=1, device_id=device, device_id_type=MESH)

    def near_peer(step):
        return base + (near ^ ((step % 4) * 8 + step // 4))

    def greet_near(step, carry):
        greet({"cube": near_peer(step)})
        return carry

    lax.fori_loop(1, HALF, greet_near, 0)
    for device in level_peers + [half_peer, {"cube": mirror}]:
        greet(device)
    for there, device in (
        (is_entry, entry_to[0]),
        (is_entry, entry_to[1]),
        (is_hub, entry_from),
    ):
        pl.when(there)(functools.partial(greet, device))

    mine = pl.ds(near * CAP, CAP)
    kept = [
        pltpu.make_async_copy(send_ref.at[mirror], far_tiles.at[mine], keep_sem.at[0]),
        pltpu.make_async_copy(slots_ref.at[mirror], far_slots.at[near], keep_sem.at[1]),
        pltpu.make_async_copy(send_ref.at[cube], near_tiles.at[mine], keep_sem.at[2]),
        pltpu.make_async_copy(slots_ref.at[cube], near_slots.at[near], keep_sem.at[3]),
        pltpu.make_async_copy(front_ref, out_ref, keep_sem.at[4]),
    ]
    for copy in kept:
        copy.start()

    pl.semaphore_wait(
        barrier,
        HALF
        + 4
        + 2 * is_entry.astype(jnp.int32)
        + is_hub.astype(jnp.int32),
    )

    def remote(source, target, send_sem, recv_sem, device):
        return pltpu.make_async_remote_copy(
            src_ref=source,
            dst_ref=target,
            send_sem=send_sem,
            recv_sem=recv_sem,
            device_id=device,
            device_id_type=MESH,
        )

    def far_copies(step):
        to = near_peer(step)
        device = {"cube": to}
        return (
            remote(
                slots_ref.at[to ^ HALF],
                far_slots.at[near],
                far_slot_send.at[step],
                far_slot_recv.at[step],
                device,
            ),
            remote(
                send_ref.at[to ^ HALF],
                far_tiles.at[mine],
                far_send.at[step],
                far_recv.at[step],
                device,
            ),
        )

    def near_copies(step):
        to = near_peer(step)
        device = {"cube": to}
        return (
            remote(
                slots_ref.at[to],
                near_slots.at[near],
                near_slot_send.at[step],
                near_slot_recv.at[step],
                device,
            ),
            remote(
                send_ref.at[to],
                near_tiles.at[mine],
                near_send.at[step],
                near_recv.at[step],
                device,
            ),
        )

    def each(copies, action):
        def body(step, carry):
            for copy in copies(step):
                getattr(copy, action)()
            return carry

        lax.fori_loop(1, HALF, body, 0)

    def sum_runs(slot_rows, tiles):
        for k, values in enumerate(sort_table(jnp.sum(slot_rows[...], axis=0))):
            table[k : k + 1] = values
        copy = pltpu.make_async_copy(table, order, table_sem.at[0])
        copy.start()
        copy.wait()

        def add(rank, run):
            tile = tiles[order[0, rank]].astype(jnp.float32)
            run = tile + jnp.where(order[1, rank] > 0, run, 0.0)
            runs[rank] = run
            return run

        lax.fori_loop(
            0, tile_count, add, jnp.zeros((height, lanes), jnp.float32), unroll=8
        )

    def block_sum(s):
        return jnp.where(order[3, s] > 0, runs[order[2, s]], 0.0)

    each(far_copies, "start")
    each(far_copies, "wait_recv")
    kept[0].wait()
    kept[1].wait()
    each(near_copies, "start")

    sum_runs(far_slots, far_tiles)
    per_row = cols // lanes
    group = width // lanes
    tile_rows = rows // height
    bursts = dense.shape[1] // BURST
    dense_copies = []
    for part in range(PARTS):

        def fill(r, carry):
            for c in range(group):
                dense[part, r * group + c] = block_sum(r * per_row + part * group + c).astype(
                    jnp.bfloat16
                )
            return carry

        lax.fori_loop(0, tile_rows, fill, 0, unroll=2)
        for k in range(bursts):
            here = pl.ds(k * BURST, BURST)
            dense_copies.append(
                remote(
                    dense.at[part, here],
                    got_dense.at[part, here],
                    dense_send.at[part, k],
                    dense_recv.at[part, k],
                    {"cube": mirror},
                )
            )
            if part < EARLY:
                dense_copies[-1].start()

    each(near_copies, "wait_recv")
    kept[2].wait()
    kept[3].wait()
    kept[4].wait()
    sum_runs(near_slots, near_tiles)

    def assemble(part):
        for copy in dense_copies[part * bursts : (part + 1) * bursts]:
            copy.wait_recv()

        def fill(r, carry):
            for c in range(group):
                here = (
                    pl.ds(pl.multiple_of(r * height, height), height),
                    pl.ds((part * group + c) * lanes, lanes),
                )
                out_ref[here] = (
                    out_ref[here]
                    + block_sum(r * per_row + part * group + c)
                    + got_dense[part, r * group + c].astype(jnp.float32)
                )
            return carry

        lax.fori_loop(0, tile_rows, fill, 0, unroll=2)

    assemble(0)

    @pl.when(is_root)
    def _():
        panel = jnp.dot(
            out_ref[:, :width].astype(jnp.bfloat16),
            diag_ref[...],
            preferred_element_type=jnp.float32,
        ).astype(jnp.bfloat16)
        for q in range(PIECES):
            own[q] = panel[q * depth : (q + 1) * depth]

    started = []

    def send(there, source, target, send_sem, recv_sem, device):
        copy = remote(source, target, send_sem, recv_sem, device)
        if there is None:
            copy.start()
        else:
            pl.when(there)(copy.start)
        started.append((there, copy))

    def arrived(target, recv_sem):
        remote(target, target, recv_sem, recv_sem, core_peer).wait_recv()

    first = jnp.maximum(z % 4 - 1, 0)
    for s in range(3):
        y_to = 1 + (first + s) % 3
        for q in range(PIECES):
            send(
                is_root,
                own.at[q],
                own.at[q],
                down_send.at[s, q],
                own_recv.at[q],
                at(z, x, core, 0, y_to),
            )

    for q in range(PIECES):
        pl.when(is_entry & (y != 0))(functools.partial(arrived, own.at[q], own_recv.at[q]))
        for k in range(2):
            send(
                is_entry,
                own.at[q],
                across.at[block, q],
                entry_send.at[q, k],
                across_recv.at[block, q],
                entry_to[k],
            )

    for step in range(PIECES + 1):
        q = step
        if q < PIECES:
            ready = across_recv.at[block, q]
            arrived(across.at[block, q], ready)
            held = (across.at[block, q], across.at[block, q])
            for s in range(3):
                send(is_hub, *held, line_send.at[q, s], ready, line_peers[s])
            for s in range(3):
                send(None, *held, row_send.at[q, s], ready, row_peers[s])
            send(None, *held, core_send.at[q, 0], ready, core_peer)
        q = step - 1
        if q >= 0:
            for s in range(3):
                theirs = ((x + s + 1) % 4) * 2 + core
                ready = across_recv.at[theirs, q]
                arrived(across.at[theirs, q], ready)
                held = (across.at[theirs, q], across.at[theirs, q])
                send(None, *held, core_send.at[q, s + 1], ready, core_peer)
        for copy in dense_copies[EARLY * bursts + step * LATE : EARLY * bursts + (step + 1) * LATE]:
            copy.start()
        if step == 2:
            for q in range(PIECES):
                pl.when((half == 0) & (y != 0) & jnp.logical_not(is_entry))(
                    functools.partial(arrived, own.at[q], own_recv.at[q])
                )
            for q in range(PIECES):
                send(
                    (half == 0) & (y == q % 4),
                    own.at[q],
                    own.at[q],
                    cross_send.at[q],
                    own_recv.at[q],
                    half_peer,
                )
        if step == PIECES:
            for q in range(PIECES):
                holds = (half == 1) & (y == q % 4)
                pl.when(holds)(functools.partial(arrived, own.at[q], own_recv.at[q]))
                for s in range(3):
                    send(
                        holds,
                        own.at[q],
                        own.at[q],
                        level_send.at[q, s],
                        own_recv.at[q],
                        level_peers[s],
                    )

    for part in range(1, PARTS):
        assemble(part)
    for q in range(PIECES):
        pl.when((half == 1) & (y != q % 4))(
            functools.partial(arrived, own.at[q], own_recv.at[q])
        )
    for q in range(PIECES):
        for s in range(4):
            theirs = s * 2 + 1 - core
            arrived(across.at[theirs, q], across_recv.at[theirs, q])

    panel = own[...].reshape(rows, width)
    span = cols // 4
    for s in range(4):
        part = across[2 * s : 2 * s + 2].reshape(span, width)
        update = lax.dot_general(
            panel, part, (((1,), (1,)), ((), ())), preferred_element_type=jnp.float32
        )
        here = slice(s * span, (s + 1) * span)
        out_ref[:, here] = out_ref[:, here] - update

    @pl.when(is_root)
    def _():
        out_ref[:, :width] = panel.astype(jnp.float32)

    each(far_copies, "wait_send")
    each(near_copies, "wait_send")
    for copy in dense_copies:
        copy.wait_send()
    for there, copy in started:
        if there is None:
            copy.wait_send()
        else:
            pl.when(there)(copy.wait_send)


def factor(send_tiles, send_slots, front, diag_inverse):
    rows, cols = front.shape
    width = diag_inverse.shape[0]
    depth = rows // PIECES
    tile = send_tiles.shape[2:]
    vmem = pl.BlockSpec(memory_space=pltpu.VMEM)
    dma = pltpu.SemaphoreType.DMA
    return pl.pallas_call(
        front_kernel,
        out_shape=jax.ShapeDtypeStruct((rows, cols), jnp.float32),
        in_specs=[vmem, vmem, pl.BlockSpec(memory_space=pl.ANY), vmem],
        out_specs=vmem,
        scratch_shapes=[
            pltpu.VMEM((HALF * CAP,) + tile, jnp.bfloat16),
            pltpu.VMEM((HALF * CAP,) + tile, jnp.bfloat16),
            pltpu.VMEM((HALF, 1, 128), jnp.int32),
            pltpu.VMEM((HALF, 1, 128), jnp.int32),
            pltpu.VMEM((HALF * CAP,) + tile, jnp.float32),
            pltpu.VMEM((8, 128), jnp.int32),
            pltpu.SMEM((8, 128), jnp.int32),
            pltpu.VMEM((PARTS, EMPTY // PARTS) + tile, jnp.bfloat16),
            pltpu.VMEM((PARTS, EMPTY // PARTS) + tile, jnp.bfloat16),
            pltpu.VMEM((PIECES, depth, width), jnp.bfloat16),
            pltpu.VMEM((BLOCKS, PIECES, depth, width), jnp.bfloat16),
            dma((1,)),
            dma((5,)),
            dma((HALF,)),
            dma((HALF,)),
            dma((HALF,)),
            dma((HALF,)),
            dma((HALF,)),
            dma((HALF,)),
            dma((HALF,)),
            dma((HALF,)),
            dma((PARTS, EMPTY // PARTS // BURST)),
            dma((PARTS, EMPTY // PARTS // BURST)),
            dma((PIECES,)),
            dma((BLOCKS, PIECES)),
            dma((3, PIECES)),
            dma((PIECES,)),
            dma((PIECES, 3)),
            dma((PIECES, 2)),
            dma((PIECES, 3)),
            dma((PIECES, 3)),
            dma((PIECES, 4)),
        ],
        compiler_params=pltpu.CompilerParams(
            collective_id=1, has_side_effects=True, vmem_limit_bytes=48 * 2**20
        ),
    )(send_tiles, send_slots, front, diag_inverse)


def local(front_matrix, child_tiles, dest_cube, dest_slot, diag_inverse):
    tile_count = child_tiles.shape[2]
    send_tiles, send_slots = pack(
        dest_cube.reshape(tile_count),
        dest_slot.reshape(tile_count),
        child_tiles.reshape(child_tiles.shape[2:]),
        lax.axis_size("cube"),
    )
    return factor(send_tiles, send_slots, front_matrix, diag_inverse)


def solution(mesh):
    in_specs = (
        P("cube", "col"),
        P("cube", "col", None, None, None),
        P("cube", "col", None, None),
        P("cube", "col", None),
        P(),
    )
    out_specs = P("cube", "col")
    return jax.shard_map(local, mesh=mesh, in_specs=in_specs, out_specs=out_specs, check_vma=False)
```

```python
import functools

import jax
import jax.numpy as jnp
from jax import lax
from jax.experimental import pallas as pl
from jax.experimental.pallas import tpu as pltpu
from jax.sharding import PartitionSpec as P

CAP = 4
EMPTY = 72
HALF = 32
PARTS = 3
MESH = pl.DeviceIdType.MESH
PIECES = 6
BURST = 4
EARLY = 12
LATE = 2
LATE_STEP = 0
ORDER = 1
CROSS_STEP = 2
LEVEL_STEP = 6
WAVES = 1
BLOCKS = 8


def pack_kernel(cube_ref, slot_ref, tiles_ref, send_ref, slots_ref, counts):
    groups = send_ref.shape[0]
    place_from = (lax.axis_index("cube") % HALF) * CAP
    lane = lax.broadcasted_iota(jnp.int32, slots_ref.shape, 2)
    slots_ref[...] = jnp.where((lane >= place_from) & (lane < place_from + CAP), EMPTY, 0)
    lane = lax.broadcasted_iota(jnp.int32, (1, slots_ref.shape[2]), 1)

    def clear(g, carry):
        counts[g] = 0
        return carry

    lax.fori_loop(0, groups, clear, 0, unroll=8)

    def place(t, carry):
        g = cube_ref[t]
        p = counts[g]
        counts[g] = p + 1
        send_ref[g, p] = tiles_ref[t]
        slots_ref[g] = jnp.where(lane == place_from + p, slot_ref[t], slots_ref[g])
        return carry

    lax.fori_loop(0, tiles_ref.shape[0], place, 0, unroll=4)


def pack(target, slot_ids, tiles, groups):
    smem = pl.BlockSpec(memory_space=pltpu.SMEM)
    vmem = pl.BlockSpec(memory_space=pltpu.VMEM)
    return pl.pallas_call(
        pack_kernel,
        out_shape=(
            jax.ShapeDtypeStruct((groups, CAP) + tiles.shape[1:], tiles.dtype),
            jax.ShapeDtypeStruct((groups, 1, 128), jnp.int32),
        ),
        in_specs=[smem, smem, vmem],
        out_specs=(vmem, vmem),
        scratch_shapes=[pltpu.SMEM((groups,), jnp.int32)],
        compiler_params=pltpu.CompilerParams(vmem_limit_bytes=40 * 2**20),
    )(target, slot_ids, tiles)


def sort_table(row):
    count = row.shape[1]
    along = jnp.broadcast_to(row, (count, count))
    i = lax.broadcasted_iota(jnp.int32, (count, count), 0)
    j = lax.broadcasted_iota(jnp.int32, (count, count), 1)

    def total(mask, value, axis):
        return jnp.sum(jnp.where(mask, value, 0), axis=axis, keepdims=True)

    down = total(i == j, along, 1)
    earlier = (along == down) & (j < i)
    rank = total((along < down) | earlier, 1, 1)
    repeats = total(earlier, 1, 1)
    hit = rank == j
    return (
        total(hit, i, 0),
        total(hit & (repeats > 0), 1, 0),
        jnp.maximum(total(down <= j, 1, 0) - 1, 0),
        total(down == j, 1, 0),
    )


def front_kernel(
    send_ref,
    slots_ref,
    front_ref,
    diag_ref,
    out_ref,
    far_tiles,
    near_tiles,
    far_slots,
    near_slots,
    runs,
    table,
    order,
    dense,
    got_dense,
    own,
    across,
    table_sem,
    keep_sem,
    far_send,
    far_recv,
    far_slot_send,
    far_slot_recv,
    near_send,
    near_recv,
    near_slot_send,
    near_slot_recv,
    dense_send,
    dense_recv,
    own_recv,
    across_recv,
    down_send,
    cross_send,
    level_send,
    entry_send,
    line_send,
    row_send,
    core_send,
):
    cube = lax.axis_index("cube")
    col = lax.axis_index("col")
    z = cube // 8
    x = (cube // 2) % 4
    core = cube % 2
    half = col // 4
    y = col % 4
    block = cube % 8
    near = cube % HALF
    base = cube - near
    mirror = cube ^ HALF
    rows, cols = front_ref.shape
    width = diag_ref.shape[0]
    depth = rows // PIECES
    tile_count, height, lanes = far_tiles.shape

    def at(z_to, x_to, core_to, half_to, y_to):
        return {"cube": z_to * 8 + x_to * 2 + core_to, "col": half_to * 4 + y_to}

    is_root = col == 0
    is_entry = (half == 0) & (y == z % 4)
    line = z - z % 4
    is_hub = z == jnp.where(z < 4, 2 - (col == 2).astype(jnp.int32), 5)
    level_peers = [at(z, x, core, half, (y + s) % 4) for s in (1, 2, 3)]
    half_peer = at(z, x, core, 1 - half, y)
    row_peers = [at(z, (x + s) % 4, core, half, y) for s in (1, 2, 3)]
    core_peer = at(z, x, 1 - core, half, y)
    line_peers = [at(line + (z + s) % 4, x, core, half, y) for s in (1, 2, 3)]
    entry_to = [
        at(hub, x, core, z // 4, y) for hub in (2 - (z == 2).astype(jnp.int32), 5)
    ]
    entry_from = at(half * 4 + y, x, core, 0, y)

    barrier = pltpu.get_barrier_semaphore()

    def greet(device):
        pl.semaphore_signal(barrier, inc=1, device_id=device, device_id_type=MESH)

    def near_peer(apart):
        return base + (near ^ apart)

    def apart_at(place):
        if not WAVES:
            return ((place + 1) % 4) * 8 + (place + 1) // 4
        place = place + jnp.where(core == 0, 1, place // 16)
        return (place % 4) * 8 + (place // 4 % 4) * 2 + (core ^ (place // 16))

    def greet_near(step, carry):
        greet({"cube": near_peer(step)})
        return carry

    lax.fori_loop(1, HALF, greet_near, 0)
    for device in level_peers + [half_peer, {"cube": mirror}]:
        greet(device)
    for there, device in (
        (is_entry, entry_to[0]),
        (is_entry, entry_to[1]),
        (is_hub, entry_from),
    ):
        pl.when(there)(functools.partial(greet, device))

    mine = pl.ds(near * CAP, CAP)
    kept = [
        pltpu.make_async_copy(send_ref.at[mirror], far_tiles.at[mine], keep_sem.at[0]),
        pltpu.make_async_copy(slots_ref.at[mirror], far_slots.at[near], keep_sem.at[1]),
        pltpu.make_async_copy(send_ref.at[cube], near_tiles.at[mine], keep_sem.at[2]),
        pltpu.make_async_copy(slots_ref.at[cube], near_slots.at[near], keep_sem.at[3]),
        pltpu.make_async_copy(front_ref, out_ref, keep_sem.at[4]),
    ]
    for copy in kept:
        copy.start()

    pl.semaphore_wait(
        barrier,
        HALF
        + 4
        + 2 * is_entry.astype(jnp.int32)
        + is_hub.astype(jnp.int32),
    )

    def remote(source, target, send_sem, recv_sem, device):
        return pltpu.make_async_remote_copy(
            src_ref=source,
            dst_ref=target,
            send_sem=send_sem,
            recv_sem=recv_sem,
            device_id=device,
            device_id_type=MESH,
        )

    def far_copies(step):
        to = near_peer(step)
        device = {"cube": to}
        return (
            remote(
                slots_ref.at[to ^ HALF],
                far_slots.at[near],
                far_slot_send.at[step],
                far_slot_recv.at[step],
                device,
            ),
            remote(
                send_ref.at[to ^ HALF],
                far_tiles.at[mine],
                far_send.at[step],
                far_recv.at[step],
                device,
            ),
        )

    def near_copies(step):
        to = near_peer(step)
        device = {"cube": to}
        return (
            remote(
                slots_ref.at[to],
                near_slots.at[near],
                near_slot_send.at[step],
                near_slot_recv.at[step],
                device,
            ),
            remote(
                send_ref.at[to],
                near_tiles.at[mine],
                near_send.at[step],
                near_recv.at[step],
                device,
            ),
        )

    def each(copies, action):
        def body(place, carry):
            for copy in copies(apart_at(place)):
                getattr(copy, action)()
            return carry

        lax.fori_loop(0, HALF - 1, body, 0)

    def sum_runs(slot_rows, tiles):
        for k, values in enumerate(sort_table(jnp.sum(slot_rows[...], axis=0))):
            table[k : k + 1] = values
        copy = pltpu.make_async_copy(table, order, table_sem.at[0])
        copy.start()
        copy.wait()

        def add(rank, run):
            tile = tiles[order[0, rank]].astype(jnp.float32)
            run = tile + jnp.where(order[1, rank] > 0, run, 0.0)
            runs[rank] = run
            return run

        lax.fori_loop(
            0, tile_count, add, jnp.zeros((height, lanes), jnp.float32), unroll=8
        )

    def block_sum(s):
        return jnp.where(order[3, s] > 0, runs[order[2, s]], 0.0)

    each(far_copies, "start")
    each(far_copies, "wait_recv")
    kept[0].wait()
    kept[1].wait()
    if ORDER == 0:
        each(near_copies, "start")

    sum_runs(far_slots, far_tiles)
    per_row = cols // lanes
    group = width // lanes
    tile_rows = rows // height
    bursts = dense.shape[1] // BURST
    dense_copies = []
    for part in range(PARTS):

        def fill(r, carry):
            for c in range(group):
                dense[part, r * group + c] = block_sum(r * per_row + part * group + c).astype(
                    jnp.bfloat16
                )
            return carry

        lax.fori_loop(0, tile_rows, fill, 0, unroll=2)
        for k in range(bursts):
            here = pl.ds(k * BURST, BURST)
            dense_copies.append(
                remote(
                    dense.at[part, here],
                    got_dense.at[part, here],
                    dense_send.at[part, k],
                    dense_recv.at[part, k],
                    {"cube": mirror},
                )
            )
            if part * bursts + k < EARLY:
                dense_copies[-1].start()
        if part + 1 == ORDER:
            each(near_copies, "start")

    each(near_copies, "wait_recv")
    kept[2].wait()
    kept[3].wait()
    kept[4].wait()
    sum_runs(near_slots, near_tiles)

    def assemble(part):
        for copy in dense_copies[part * bursts : (part + 1) * bursts]:
            copy.wait_recv()

        def fill(r, carry):
            for c in range(group):
                here = (
                    pl.ds(pl.multiple_of(r * height, height), height),
                    pl.ds((part * group + c) * lanes, lanes),
                )
                out_ref[here] = (
                    out_ref[here]
                    + block_sum(r * per_row + part * group + c)
                    + got_dense[part, r * group + c].astype(jnp.float32)
                )
            return carry

        lax.fori_loop(0, tile_rows, fill, 0, unroll=2)

    assemble(0)

    @pl.when(is_root)
    def _():
        panel = jnp.dot(
            out_ref[:, :width].astype(jnp.bfloat16),
            diag_ref[...],
            preferred_element_type=jnp.float32,
        ).astype(jnp.bfloat16)
        for q in range(PIECES):
            own[q] = panel[q * depth : (q + 1) * depth]

    started = []

    def send(there, source, target, send_sem, recv_sem, device):
        copy = remote(source, target, send_sem, recv_sem, device)
        if there is None:
            copy.start()
        else:
            pl.when(there)(copy.start)
        started.append((there, copy))

    def arrived(target, recv_sem):
        remote(target, target, recv_sem, recv_sem, core_peer).wait_recv()

    first = jnp.maximum(z % 4 - 1, 0)
    for s in range(3):
        y_to = 1 + (first + s) % 3
        for q in range(PIECES):
            send(
                is_root,
                own.at[q],
                own.at[q],
                down_send.at[s, q],
                own_recv.at[q],
                at(z, x, core, 0, y_to),
            )

    for q in range(PIECES):
        pl.when(is_entry & (y != 0))(functools.partial(arrived, own.at[q], own_recv.at[q]))
        for k in range(2):
            send(
                is_entry,
                own.at[q],
                across.at[block, q],
                entry_send.at[q, k],
                across_recv.at[block, q],
                entry_to[k],
            )

    for step in range(PIECES + 1):
        q = step
        if q < PIECES:
            ready = across_recv.at[block, q]
            arrived(across.at[block, q], ready)
            held = (across.at[block, q], across.at[block, q])
            for s in range(3):
                send(is_hub, *held, line_send.at[q, s], ready, line_peers[s])
            for s in range(3):
                send(None, *held, row_send.at[q, s], ready, row_peers[s])
            send(None, *held, core_send.at[q, 0], ready, core_peer)
        q = step - 1
        if q >= 0:
            for s in range(3):
                theirs = ((x + s + 1) % 4) * 2 + core
                ready = across_recv.at[theirs, q]
                arrived(across.at[theirs, q], ready)
                held = (across.at[theirs, q], across.at[theirs, q])
                send(None, *held, core_send.at[q, s + 1], ready, core_peer)
        if step >= LATE_STEP:
            late = EARLY + (step - LATE_STEP) * LATE
            for copy in dense_copies[late : late + LATE]:
                copy.start()
        if step == CROSS_STEP:
            for q in range(PIECES):
                pl.when((half == 0) & (y != 0) & jnp.logical_not(is_entry))(
                    functools.partial(arrived, own.at[q], own_recv.at[q])
                )
            for q in range(PIECES):
                send(
                    (half == 0) & (y == q % 4),
                    own.at[q],
                    own.at[q],
                    cross_send.at[q],
                    own_recv.at[q],
                    half_peer,
                )
        if step == LEVEL_STEP:
            for q in range(PIECES):
                holds = (half == 1) & (y == q % 4)
                pl.when(holds)(functools.partial(arrived, own.at[q], own_recv.at[q]))
                for s in range(3):
                    send(
                        holds,
                        own.at[q],
                        own.at[q],
                        level_send.at[q, s],
                        own_recv.at[q],
                        level_peers[s],
                    )

    for part in range(1, PARTS):
        assemble(part)
    for q in range(PIECES):
        pl.when((half == 1) & (y != q % 4))(
            functools.partial(arrived, own.at[q], own_recv.at[q])
        )
    for q in range(PIECES):
        for s in range(4):
            theirs = s * 2 + 1 - core
            arrived(across.at[theirs, q], across_recv.at[theirs, q])

    panel = own[...].reshape(rows, width)
    span = cols // 4
    for s in range(4):
        part = across[2 * s : 2 * s + 2].reshape(span, width)
        update = lax.dot_general(
            panel, part, (((1,), (1,)), ((), ())), preferred_element_type=jnp.float32
        )
        here = slice(s * span, (s + 1) * span)
        out_ref[:, here] = out_ref[:, here] - update

    @pl.when(is_root)
    def _():
        out_ref[:, :width] = panel.astype(jnp.float32)

    each(far_copies, "wait_send")
    each(near_copies, "wait_send")
    for copy in dense_copies:
        copy.wait_send()
    for there, copy in started:
        if there is None:
            copy.wait_send()
        else:
            pl.when(there)(copy.wait_send)


def factor(send_tiles, send_slots, front, diag_inverse):
    rows, cols = front.shape
    width = diag_inverse.shape[0]
    depth = rows // PIECES
    tile = send_tiles.shape[2:]
    vmem = pl.BlockSpec(memory_space=pltpu.VMEM)
    dma = pltpu.SemaphoreType.DMA
    return pl.pallas_call(
        front_kernel,
        out_shape=jax.ShapeDtypeStruct((rows, cols), jnp.float32),
        in_specs=[vmem, vmem, pl.BlockSpec(memory_space=pl.ANY), vmem],
        out_specs=vmem,
        scratch_shapes=[
            pltpu.VMEM((HALF * CAP,) + tile, jnp.bfloat16),
            pltpu.VMEM((HALF * CAP,) + tile, jnp.bfloat16),
            pltpu.VMEM((HALF, 1, 128), jnp.int32),
            pltpu.VMEM((HALF, 1, 128), jnp.int32),
            pltpu.VMEM((HALF * CAP,) + tile, jnp.float32),
            pltpu.VMEM((8, 128), jnp.int32),
            pltpu.SMEM((8, 128), jnp.int32),
            pltpu.VMEM((PARTS, EMPTY // PARTS) + tile, jnp.bfloat16),
            pltpu.VMEM((PARTS, EMPTY // PARTS) + tile, jnp.bfloat16),
            pltpu.VMEM((PIECES, depth, width), jnp.bfloat16),
            pltpu.VMEM((BLOCKS, PIECES, depth, width), jnp.bfloat16),
            dma((1,)),
            dma((5,)),
            dma((HALF,)),
            dma((HALF,)),
            dma((HALF,)),
            dma((HALF,)),
            dma((HALF,)),
            dma((HALF,)),
            dma((HALF,)),
            dma((HALF,)),
            dma((PARTS, EMPTY // PARTS // BURST)),
            dma((PARTS, EMPTY // PARTS // BURST)),
            dma((PIECES,)),
            dma((BLOCKS, PIECES)),
            dma((3, PIECES)),
            dma((PIECES,)),
            dma((PIECES, 3)),
            dma((PIECES, 2)),
            dma((PIECES, 3)),
            dma((PIECES, 3)),
            dma((PIECES, 4)),
        ],
        compiler_params=pltpu.CompilerParams(
            collective_id=1, has_side_effects=True, vmem_limit_bytes=48 * 2**20
        ),
    )(send_tiles, send_slots, front, diag_inverse)


def local(front_matrix, child_tiles, dest_cube, dest_slot, diag_inverse):
    tile_count = child_tiles.shape[2]
    send_tiles, send_slots = pack(
        dest_cube.reshape(tile_count),
        dest_slot.reshape(tile_count),
        child_tiles.reshape(child_tiles.shape[2:]),
        lax.axis_size("cube"),
    )
    return factor(send_tiles, send_slots, front_matrix, diag_inverse)


def solution(mesh):
    in_specs = (
        P("cube", "col"),
        P("cube", "col", None, None, None),
        P("cube", "col", None, None),
        P("cube", "col", None),
        P(),
    )
    out_specs = P("cube", "col")
    return jax.shard_map(local, mesh=mesh, in_specs=in_specs, out_specs=out_specs, check_vma=False)
```

```python
import functools

import jax
import jax.numpy as jnp
from jax import lax
from jax.experimental import pallas as pl
from jax.experimental.pallas import tpu as pltpu
from jax.sharding import PartitionSpec as P

CAP = 4
EMPTY = 72
HALF = 32
PARTS = 3
MESH = pl.DeviceIdType.MESH
PIECES = 6
BURST = 4
EARLY = 12
LATE = 2
LATE_STEP = 0
ORDER = 1
CROSS_STEP = 2
LEVEL_STEP = 6
WAVES = 1
BLOCKS = 8


def pack_kernel(cube_ref, slot_ref, tiles_ref, send_ref, slots_ref, counts):
    groups = send_ref.shape[0]
    place_from = (lax.axis_index("cube") % HALF) * CAP
    lane = lax.broadcasted_iota(jnp.int32, slots_ref.shape, 2)
    slots_ref[...] = jnp.where((lane >= place_from) & (lane < place_from + CAP), EMPTY, 0)
    lane = lax.broadcasted_iota(jnp.int32, (1, slots_ref.shape[2]), 1)

    def clear(g, carry):
        counts[g] = 0
        return carry

    lax.fori_loop(0, groups, clear, 0, unroll=8)

    def place(t, carry):
        g = cube_ref[t]
        p = counts[g]
        counts[g] = p + 1
        send_ref[g, p] = tiles_ref[t]
        slots_ref[g] = jnp.where(lane == place_from + p, slot_ref[t], slots_ref[g])
        return carry

    lax.fori_loop(0, tiles_ref.shape[0], place, 0, unroll=4)


def pack(target, slot_ids, tiles, groups):
    smem = pl.BlockSpec(memory_space=pltpu.SMEM)
    vmem = pl.BlockSpec(memory_space=pltpu.VMEM)
    return pl.pallas_call(
        pack_kernel,
        out_shape=(
            jax.ShapeDtypeStruct((groups, CAP) + tiles.shape[1:], tiles.dtype),
            jax.ShapeDtypeStruct((groups, 1, 128), jnp.int32),
        ),
        in_specs=[smem, smem, vmem],
        out_specs=(vmem, vmem),
        scratch_shapes=[pltpu.SMEM((groups,), jnp.int32)],
        compiler_params=pltpu.CompilerParams(vmem_limit_bytes=40 * 2**20),
    )(target, slot_ids, tiles)


def sort_table(row):
    count = row.shape[1]
    along = jnp.broadcast_to(row, (count, count))
    i = lax.broadcasted_iota(jnp.int32, (count, count), 0)
    j = lax.broadcasted_iota(jnp.int32, (count, count), 1)

    def total(mask, value, axis):
        return jnp.sum(jnp.where(mask, value, 0), axis=axis, keepdims=True)

    down = total(i == j, along, 1)
    earlier = (along == down) & (j < i)
    rank = total((along < down) | earlier, 1, 1)
    repeats = total(earlier, 1, 1)
    hit = rank == j
    return (
        total(hit, i, 0),
        total(hit & (repeats > 0), 1, 0),
        jnp.maximum(total(down <= j, 1, 0) - 1, 0),
        total(down == j, 1, 0),
    )


def front_kernel(
    send_ref,
    slots_ref,
    front_ref,
    diag_ref,
    out_ref,
    far_tiles,
    near_tiles,
    far_slots,
    near_slots,
    runs,
    table,
    order,
    dense,
    got_dense,
    own,
    across,
    table_sem,
    keep_sem,
    far_send,
    far_recv,
    far_slot_send,
    far_slot_recv,
    near_send,
    near_recv,
    near_slot_send,
    near_slot_recv,
    dense_send,
    dense_recv,
    own_recv,
    across_recv,
    down_send,
    cross_send,
    level_send,
    entry_send,
    line_send,
    row_send,
    core_send,
):
    cube = lax.axis_index("cube")
    col = lax.axis_index("col")
    z = cube // 8
    x = (cube // 2) % 4
    core = cube % 2
    half = col // 4
    y = col % 4
    block = cube % 8
    near = cube % HALF
    base = cube - near
    mirror = cube ^ HALF
    rows, cols = front_ref.shape
    width = diag_ref.shape[0]
    depth = rows // PIECES
    tile_count, height, lanes = far_tiles.shape

    def at(z_to, x_to, core_to, half_to, y_to):
        return {"cube": z_to * 8 + x_to * 2 + core_to, "col": half_to * 4 + y_to}

    is_root = col == 0
    is_entry = (half == 0) & (y == z % 4)
    line = z - z % 4
    is_hub = z == jnp.where(z < 4, 2 - (col == 2).astype(jnp.int32), 5)
    level_peers = [at(z, x, core, half, (y + s) % 4) for s in (1, 2, 3)]
    half_peer = at(z, x, core, 1 - half, y)
    row_peers = [at(z, (x + s) % 4, core, half, y) for s in (1, 2, 3)]
    core_peer = at(z, x, 1 - core, half, y)
    line_peers = [at(line + (z + s) % 4, x, core, half, y) for s in (1, 2, 3)]
    entry_to = [
        at(hub, x, core, z // 4, y) for hub in (2 - (z == 2).astype(jnp.int32), 5)
    ]
    entry_from = at(half * 4 + y, x, core, 0, y)

    barrier = pltpu.get_barrier_semaphore()

    def greet(device):
        pl.semaphore_signal(barrier, inc=1, device_id=device, device_id_type=MESH)

    def near_peer(apart):
        return base + (near ^ apart)

    def apart_at(place):
        if not WAVES:
            return ((place + 1) % 4) * 8 + (place + 1) // 4
        place = place + jnp.where(core == 0, 1, place // 16)
        return (place % 4) * 8 + (place // 4 % 4) * 2 + (core ^ (place // 16))

    def greet_near(step, carry):
        greet({"cube": near_peer(step)})
        return carry

    lax.fori_loop(1, HALF, greet_near, 0)
    for device in level_peers + [half_peer, {"cube": mirror}]:
        greet(device)
    for there, device in (
        (is_entry, entry_to[0]),
        (is_entry, entry_to[1]),
        (is_hub, entry_from),
    ):
        pl.when(there)(functools.partial(greet, device))

    mine = pl.ds(near * CAP, CAP)
    kept = [
        pltpu.make_async_copy(send_ref.at[mirror], far_tiles.at[mine], keep_sem.at[0]),
        pltpu.make_async_copy(slots_ref.at[mirror], far_slots.at[near], keep_sem.at[1]),
        pltpu.make_async_copy(send_ref.at[cube], near_tiles.at[mine], keep_sem.at[2]),
        pltpu.make_async_copy(slots_ref.at[cube], near_slots.at[near], keep_sem.at[3]),
        pltpu.make_async_copy(front_ref, out_ref, keep_sem.at[4]),
    ]
    for copy in kept:
        copy.start()

    pl.semaphore_wait(
        barrier,
        HALF
        + 4
        + 2 * is_entry.astype(jnp.int32)
        + is_hub.astype(jnp.int32),
    )

    def remote(source, target, send_sem, recv_sem, device):
        return pltpu.make_async_remote_copy(
            src_ref=source,
            dst_ref=target,
            send_sem=send_sem,
            recv_sem=recv_sem,
            device_id=device,
            device_id_type=MESH,
        )

    def far_copies(step):
        to = near_peer(step)
        device = {"cube": to}
        return (
            remote(
                slots_ref.at[to ^ HALF],
                far_slots.at[near],
                far_slot_send.at[step],
                far_slot_recv.at[step],
                device,
            ),
            remote(
                send_ref.at[to ^ HALF],
                far_tiles.at[mine],
                far_send.at[step],
                far_recv.at[step],
                device,
            ),
        )

    def near_copies(step):
        to = near_peer(step)
        device = {"cube": to}
        return (
            remote(
                slots_ref.at[to],
                near_slots.at[near],
                near_slot_send.at[step],
                near_slot_recv.at[step],
                device,
            ),
            remote(
                send_ref.at[to],
                near_tiles.at[mine],
                near_send.at[step],
                near_recv.at[step],
                device,
            ),
        )

    def each(copies, action):
        def body(place, carry):
            for copy in copies(apart_at(place)):
                getattr(copy, action)()
            return carry

        lax.fori_loop(0, HALF - 1, body, 0)

    def sum_runs(slot_rows, tiles):
        for k, values in enumerate(sort_table(jnp.sum(slot_rows[...], axis=0))):
            table[k : k + 1] = values
        copy = pltpu.make_async_copy(table, order, table_sem.at[0])
        copy.start()
        copy.wait()

        def add(rank, run):
            tile = tiles[order[0, rank]].astype(jnp.float32)
            run = tile + jnp.where(order[1, rank] > 0, run, 0.0)
            runs[rank] = run
            return run

        lax.fori_loop(
            0, tile_count, add, jnp.zeros((height, lanes), jnp.float32), unroll=8
        )

    def block_sum(s):
        return jnp.where(order[3, s] > 0, runs[order[2, s]], 0.0)

    each(far_copies, "start")
    each(far_copies, "wait_recv")
    kept[0].wait()
    kept[1].wait()
    if ORDER == 0:
        each(near_copies, "start")

    sum_runs(far_slots, far_tiles)
    per_row = cols // lanes
    group = width // lanes
    tile_rows = rows // height
    bursts = dense.shape[1] // BURST
    dense_copies = []
    for part in range(PARTS):

        def fill(r, carry):
            for c in range(group):
                dense[part, r * group + c] = block_sum(r * per_row + part * group + c).astype(
                    jnp.bfloat16
                )
            return carry

        lax.fori_loop(0, tile_rows, fill, 0, unroll=2)
        for k in range(bursts):
            here = pl.ds(k * BURST, BURST)
            dense_copies.append(
                remote(
                    dense.at[part, here],
                    got_dense.at[part, here],
                    dense_send.at[part, k],
                    dense_recv.at[part, k],
                    {"cube": mirror},
                )
            )
            if part * bursts + k < EARLY:
                dense_copies[-1].start()
        if part + 1 == ORDER:
            each(near_copies, "start")

    each(near_copies, "wait_recv")
    kept[2].wait()
    kept[3].wait()
    kept[4].wait()
    sum_runs(near_slots, near_tiles)

    def assemble(part):
        for copy in dense_copies[part * bursts : (part + 1) * bursts]:
            copy.wait_recv()

        def fill(r, carry):
            for c in range(group):
                here = (
                    pl.ds(pl.multiple_of(r * height, height), height),
                    pl.ds((part * group + c) * lanes, lanes),
                )
                out_ref[here] = (
                    out_ref[here]
                    + block_sum(r * per_row + part * group + c)
                    + got_dense[part, r * group + c].astype(jnp.float32)
                )
            return carry

        lax.fori_loop(0, tile_rows, fill, 0, unroll=2)

    assemble(0)

    @pl.when(is_root)
    def _():
        panel = jnp.dot(
            out_ref[:, :width].astype(jnp.bfloat16),
            diag_ref[...],
            preferred_element_type=jnp.float32,
        ).astype(jnp.bfloat16)
        for q in range(PIECES):
            own[q] = panel[q * depth : (q + 1) * depth]

    started = []

    def send(there, source, target, send_sem, recv_sem, device):
        copy = remote(source, target, send_sem, recv_sem, device)
        if there is None:
            copy.start()
        else:
            pl.when(there)(copy.start)
        started.append((there, copy))

    def arrived(target, recv_sem):
        remote(target, target, recv_sem, recv_sem, core_peer).wait_recv()

    first = jnp.maximum(z % 4 - 1, 0)
    for s in range(3):
        y_to = 1 + (first + s) % 3
        for q in range(PIECES):
            send(
                is_root,
                own.at[q],
                own.at[q],
                down_send.at[s, q],
                own_recv.at[q],
                at(z, x, core, 0, y_to),
            )

    for q in range(PIECES):
        pl.when(is_entry & (y != 0))(functools.partial(arrived, own.at[q], own_recv.at[q]))
        for k in range(2):
            send(
                is_entry,
                own.at[q],
                across.at[block, q],
                entry_send.at[q, k],
                across_recv.at[block, q],
                entry_to[k],
            )

    assemble(1)
    for step in range(PIECES + 1):
        q = step
        if q < PIECES:
            ready = across_recv.at[block, q]
            arrived(across.at[block, q], ready)
            held = (across.at[block, q], across.at[block, q])
            for s in range(3):
                send(is_hub, *held, line_send.at[q, s], ready, line_peers[s])
            for s in range(3):
                send(None, *held, row_send.at[q, s], ready, row_peers[s])
            send(None, *held, core_send.at[q, 0], ready, core_peer)
        q = step - 1
        if q >= 0:
            for s in range(3):
                theirs = ((x + s + 1) % 4) * 2 + core
                ready = across_recv.at[theirs, q]
                arrived(across.at[theirs, q], ready)
                held = (across.at[theirs, q], across.at[theirs, q])
                send(None, *held, core_send.at[q, s + 1], ready, core_peer)
        if step >= LATE_STEP:
            late = EARLY + (step - LATE_STEP) * LATE
            for copy in dense_copies[late : late + LATE]:
                copy.start()
        if step == CROSS_STEP:
            for q in range(PIECES):
                pl.when((half == 0) & (y != 0) & jnp.logical_not(is_entry))(
                    functools.partial(arrived, own.at[q], own_recv.at[q])
                )
            for q in range(PIECES):
                send(
                    (half == 0) & (y == q % 4),
                    own.at[q],
                    own.at[q],
                    cross_send.at[q],
                    own_recv.at[q],
                    half_peer,
                )
        if step == LEVEL_STEP:
            for q in range(PIECES):
                holds = (half == 1) & (y == q % 4)
                pl.when(holds)(functools.partial(arrived, own.at[q], own_recv.at[q]))
                for s in range(3):
                    send(
                        holds,
                        own.at[q],
                        own.at[q],
                        level_send.at[q, s],
                        own_recv.at[q],
                        level_peers[s],
                    )

    for part in range(2, PARTS):
        assemble(part)
    for q in range(PIECES):
        pl.when((half == 1) & (y != q % 4))(
            functools.partial(arrived, own.at[q], own_recv.at[q])
        )
    for q in range(PIECES):
        for s in range(4):
            theirs = s * 2 + 1 - core
            arrived(across.at[theirs, q], across_recv.at[theirs, q])

    panel = own[...].reshape(rows, width)
    span = cols // 4
    for s in range(4):
        part = across[2 * s : 2 * s + 2].reshape(span, width)
        update = lax.dot_general(
            panel, part, (((1,), (1,)), ((), ())), preferred_element_type=jnp.float32
        )
        here = slice(s * span, (s + 1) * span)
        out_ref[:, here] = out_ref[:, here] - update

    @pl.when(is_root)
    def _():
        out_ref[:, :width] = panel.astype(jnp.float32)

    each(far_copies, "wait_send")
    each(near_copies, "wait_send")
    for copy in dense_copies:
        copy.wait_send()
    for there, copy in started:
        if there is None:
            copy.wait_send()
        else:
            pl.when(there)(copy.wait_send)


def factor(send_tiles, send_slots, front, diag_inverse):
    rows, cols = front.shape
    width = diag_inverse.shape[0]
    depth = rows // PIECES
    tile = send_tiles.shape[2:]
    vmem = pl.BlockSpec(memory_space=pltpu.VMEM)
    dma = pltpu.SemaphoreType.DMA
    return pl.pallas_call(
        front_kernel,
        out_shape=jax.ShapeDtypeStruct((rows, cols), jnp.float32),
        in_specs=[vmem, vmem, pl.BlockSpec(memory_space=pl.ANY), vmem],
        out_specs=vmem,
        scratch_shapes=[
            pltpu.VMEM((HALF * CAP,) + tile, jnp.bfloat16),
            pltpu.VMEM((HALF * CAP,) + tile, jnp.bfloat16),
            pltpu.VMEM((HALF, 1, 128), jnp.int32),
            pltpu.VMEM((HALF, 1, 128), jnp.int32),
            pltpu.VMEM((HALF * CAP,) + tile, jnp.float32),
            pltpu.VMEM((8, 128), jnp.int32),
            pltpu.SMEM((8, 128), jnp.int32),
            pltpu.VMEM((PARTS, EMPTY // PARTS) + tile, jnp.bfloat16),
            pltpu.VMEM((PARTS, EMPTY // PARTS) + tile, jnp.bfloat16),
            pltpu.VMEM((PIECES, depth, width), jnp.bfloat16),
            pltpu.VMEM((BLOCKS, PIECES, depth, width), jnp.bfloat16),
            dma((1,)),
            dma((5,)),
            dma((HALF,)),
            dma((HALF,)),
            dma((HALF,)),
            dma((HALF,)),
            dma((HALF,)),
            dma((HALF,)),
            dma((HALF,)),
            dma((HALF,)),
            dma((PARTS, EMPTY // PARTS // BURST)),
            dma((PARTS, EMPTY // PARTS // BURST)),
            dma((PIECES,)),
            dma((BLOCKS, PIECES)),
            dma((3, PIECES)),
            dma((PIECES,)),
            dma((PIECES, 3)),
            dma((PIECES, 2)),
            dma((PIECES, 3)),
            dma((PIECES, 3)),
            dma((PIECES, 4)),
        ],
        compiler_params=pltpu.CompilerParams(
            collective_id=1, has_side_effects=True, vmem_limit_bytes=48 * 2**20
        ),
    )(send_tiles, send_slots, front, diag_inverse)


def local(front_matrix, child_tiles, dest_cube, dest_slot, diag_inverse):
    tile_count = child_tiles.shape[2]
    send_tiles, send_slots = pack(
        dest_cube.reshape(tile_count),
        dest_slot.reshape(tile_count),
        child_tiles.reshape(child_tiles.shape[2:]),
        lax.axis_size("cube"),
    )
    return factor(send_tiles, send_slots, front_matrix, diag_inverse)


def solution(mesh):
    in_specs = (
        P("cube", "col"),
        P("cube", "col", None, None, None),
        P("cube", "col", None, None),
        P("cube", "col", None),
        P(),
    )
    out_specs = P("cube", "col")
    return jax.shard_map(local, mesh=mesh, in_specs=in_specs, out_specs=out_specs, check_vma=False)
```
